32 devices in a mesh: gx: 2 (over x), gy: 4 (over y, core), gz: 4 (over z).
Axes of the slice: x: 2, y: 2, z: 4, core: 2. Of those that a mesh axis runs over, the one named last changes fastest.
Arguments:
- rhs: bfloat16 [16, 32768], P(None, ('gx', 'gy', 'gz')), may hold values from -6 to 6
- leaf_basis: bfloat16 [128, 64, 256], P(('gx', 'gy', 'gz')), may hold values from -0.375 to 0.375
- leaf_transfer: bfloat16 [128, 64, 64], P(('gx', 'gy', 'gz')), may hold values from -0.375 to 0.375
- leaf_coupling: bfloat16 [128, 6, 64, 64], P(('gx', 'gy', 'gz')), may hold values from -0.3125 to 0.3125
- coupling_sources: int32 [128, 6], P(('gx', 'gy', 'gz')), may hold values from -1 to 127, as said below
- near_tiles: bfloat16 [128, 3, 256, 256], P(('gx', 'gy', 'gz')), may hold values from -0.21875 to 0.21875
- near_sources: int32 [128, 3], P(('gx', 'gy', 'gz')), may hold values from -1 to 127, as said below
- top_transfer: bfloat16 [4, 2, 64, 64], replicated, may hold values from -0.625 to 0.625
- cluster_coupling: bfloat16 [5, 2, 64, 64], replicated, may hold values from -0.5 to 0.5
Outputs:
- product: bfloat16 [16, 32768], P(None, ('gx', 'gy', 'gz'))
The draws below stay inside these ranges and needn't reach their ends.
Inputs may be any that keep to these rules, and one draw needn't show every extreme that they name: `near_sources`: slot 0 of each leaf is the leaf itself; every other entry is -1 (no block) or a leaf at most 2 places from its target leaf in the global order. `coupling_sources`: each entry is -1 (no block) or a leaf other than the target, at most 2 places from it in the global order.
All inputs are finite; a program needn't handle non-finite values.
Results may differ from the reference program's by a relative error of at most 0.0043.
Values may be sent and summed in bfloat16 or wider, within the bound.
A program may use at most 64 MiB of HBM per device.

```python
import jax
import jax.numpy as jnp
from jax import lax

LEAF = 256
RANK = 64
NRHS = 16
NEAR = 3
ADM = 6
TOPL = 4
LEAF_DEV = 4
REACH = 2
LEAVES = 128
UNKNOWNS = 32768
DEVICES = 32


def local_sources(key, slots, first_self):
    offset_key, keep_key = jax.random.split(key)
    target = jnp.arange(LEAVES, dtype=jnp.int32)[:, None]
    if first_self:
        offset = jax.random.randint(offset_key, (LEAVES, slots), -REACH, REACH + 1)
    else:
        offset = jax.random.randint(offset_key, (LEAVES, slots), -REACH, REACH)
        offset = jnp.where(offset >= 0, offset + 1, offset)
    source = target + offset.astype(jnp.int32)
    keep_slot = jax.random.randint(keep_key, (LEAVES, slots), 0, 4) > 0
    inside = (source >= 0) & (source < LEAVES)
    source = jnp.where(keep_slot & inside, source, -1)
    if first_self:
        source = source.at[:, 0].set(target[:, 0])
        after_slot = 1
        before_slot = 2
    else:
        after_slot = 0
        before_slot = 1
    leaf_pos = target[:, 0] % LEAF_DEV
    after_leaf = target[:, 0] + 1
    before_leaf = target[:, 0] - 1
    need_after = (leaf_pos == LEAF_DEV - 1) & (after_leaf < LEAVES)
    need_before = (leaf_pos == 0) & (before_leaf >= 0)
    source = source.at[:, after_slot].set(jnp.where(need_after, after_leaf, source[:, after_slot]))
    source = source.at[:, before_slot].set(jnp.where(need_before, before_leaf, source[:, before_slot]))
    source = source.at[0, slots - 1].set(-1)
    return source.astype(jnp.int32)


def draw_near_sources(key, part):
    key = jax.random.fold_in(key, 11)
    return local_sources(key, NEAR, True)


def draw_coupling_sources(key, part):
    key = jax.random.fold_in(key, 12)
    return local_sources(key, ADM, False)


def shard_levels(key, shape, cuts, smallest, top_value):
    level = 1.0
    for dim, blocks in cuts:
        steps = jax.random.uniform(jax.random.fold_in(jax.random.fold_in(key, 6), dim), (blocks,), jnp.float32, smallest / len(cuts), top_value / len(cuts))
        level = level * jnp.repeat(jnp.exp(steps), shape[dim] // blocks).reshape((-1,) + (1,) * (len(shape) - 1 - dim))
    return level


def bell_draw(key, extent, scale, limit, cuts=(), kind=jnp.bfloat16):
    values = scale * jax.random.normal(key, extent, jnp.float32)
    if cuts:
        values = values * shard_levels(key, extent, cuts, -0.22, 0.18)
    return jnp.clip(values, -limit, limit).astype(kind)


def setup_inputs(seed: int = 0) -> dict:
    seeds = jax.random.split(jax.random.key(seed), 10)
    rhs = bell_draw(seeds[0], (NRHS, UNKNOWNS), 1.0, 6.0, ((1, 32),))
    leaf_basis = bell_draw(seeds[1], (LEAVES, RANK, LEAF), LEAF ** -0.5, 0.375, ((0, 32),))
    leaf_transfer = bell_draw(seeds[2], (LEAVES, RANK, RANK), (RANK * LEAF_DEV) ** -0.5, 0.375, ((0, 32),))
    leaf_coupling = bell_draw(seeds[3], (LEAVES, ADM, RANK, RANK), (RANK * ADM) ** -0.5, 0.3125, ((0, 32),))
    coupling_sources = draw_coupling_sources(jax.random.fold_in(seeds[9], 71), 0)
    near_tiles = bell_draw(seeds[5], (LEAVES, NEAR, LEAF, LEAF), (LEAF * NEAR) ** -0.5, 0.21875, ((0, 32),))
    near_sources = draw_near_sources(jax.random.fold_in(seeds[9], 71), 0)
    top_transfer = bell_draw(seeds[7], (TOPL, 2, RANK, RANK), (RANK * 3 // 2) ** -0.5, 0.625)
    cluster_coupling = bell_draw(seeds[8], (TOPL + 1, 2, RANK, RANK), (2 * RANK) ** -0.5, 0.5)
    return {"rhs": rhs, "leaf_basis": leaf_basis, "leaf_transfer": leaf_transfer, "leaf_coupling": leaf_coupling, "coupling_sources": coupling_sources, "near_tiles": near_tiles, "near_sources": near_sources, "top_transfer": top_transfer, "cluster_coupling": cluster_coupling}


def reference(rhs, leaf_basis, leaf_transfer, leaf_coupling, coupling_sources, near_tiles, near_sources, top_transfer, cluster_coupling):
    exact = lax.Precision.HIGHEST
    blocks = rhs.reshape(NRHS, LEAVES, LEAF)
    coeffs = jnp.einsum('rts,tks->trk', blocks.astype(jnp.float32), leaf_basis.astype(jnp.float32), precision=exact).astype(jnp.bfloat16)
    usable = coupling_sources >= 0
    picked = coeffs[jnp.clip(coupling_sources, 0, LEAVES - 1).astype(jnp.int32)]
    picked = jnp.where(usable[:, :, None, None], picked, jnp.zeros((), jnp.bfloat16))
    leaf_field = jnp.einsum('tark,takm->trm', picked.astype(jnp.float32), leaf_coupling.astype(jnp.float32), precision=exact)
    grouped = coeffs.reshape(DEVICES, LEAF_DEV, NRHS, RANK).astype(jnp.float32)
    leaf_mats = leaf_transfer.reshape(DEVICES, LEAF_DEV, RANK, RANK).astype(jnp.float32)
    device_level = jnp.einsum('dlrk,dlkm->drm', grouped, leaf_mats, precision=exact)
    up_mats = top_transfer.astype(jnp.float32)
    coupling_mats = cluster_coupling.astype(jnp.float32)
    climbed = [device_level]
    for height in range(TOPL):
        before = climbed[-1]
        pairs = before.reshape(before.shape[0] // 2, 2, NRHS, RANK)
        climbed.append(jnp.einsum('gprk,pkm->grm', pairs, up_mats[height], precision=exact))
    fields = []
    for height in range(TOPL + 1):
        values = climbed[height]
        zero_row = jnp.zeros_like(values[:1])
        lower_side = jnp.concatenate([zero_row, values[:-1]], 0)
        upper_side = jnp.concatenate([values[1:], zero_row], 0)
        fields.append(jnp.einsum('grk,km->grm', lower_side, coupling_mats[height, 0], precision=exact)
                      + jnp.einsum('grk,km->grm', upper_side, coupling_mats[height, 1], precision=exact))
    incoming = fields[TOPL]
    for height in range(TOPL, 0, -1):
        lowered = jnp.einsum('grm,pkm->gprk', incoming, up_mats[height - 1], precision=exact)
        incoming = fields[height - 1] + lowered.reshape(-1, NRHS, RANK)
    spread = jnp.einsum('drm,dlkm->dlrk', incoming, leaf_mats, precision=exact).reshape(LEAVES, NRHS, RANK)
    potential = (leaf_field + spread).astype(jnp.bfloat16)
    far_part = jnp.einsum('trk,tks->rts', potential.astype(jnp.float32), leaf_basis.astype(jnp.float32), precision=exact)

    def near_block(operands):
        tiles, sources = operands
        fetched = jnp.take(blocks, jnp.clip(sources, 0, LEAVES - 1).astype(jnp.int32), axis=1)
        fetched = jnp.where((sources >= 0)[None, :, :, None], fetched, jnp.zeros((), jnp.bfloat16))
        return jnp.einsum('rtns,tnsu->tru', fetched.astype(jnp.float32), tiles.astype(jnp.float32), precision=exact)

    near_part = lax.map(near_block, (near_tiles.reshape(DEVICES, LEAF_DEV, NEAR, LEAF, LEAF),
                                     near_sources.reshape(DEVICES, LEAF_DEV, NEAR)))
    near_part = near_part.reshape(LEAVES, NRHS, LEAF).transpose(1, 0, 2)
    return (far_part + near_part).reshape(NRHS, UNKNOWNS).astype(jnp.bfloat16)
```

```python
import functools

import jax
import jax.numpy as jnp
from jax import lax
from jax.experimental import pallas as pl
from jax.experimental.pallas import tpu as pltpu
from jax.sharding import PartitionSpec as P

AXES = ("gx", "gy", "gz")
REACH = 2
MESH = pl.DeviceIdType.MESH
BF16 = jnp.bfloat16
F32 = jnp.float32


def mm(a, b):
    return jnp.dot(a, b, preferred_element_type=F32)


def mm_nt(a, b):
    return lax.dot_general(a, b, (((1,), (1,)), ((), ())), preferred_element_type=F32)


def mm_tn(a, b):
    return lax.dot_general(a, b, (((0,), (0,)), ((), ())), preferred_element_type=F32)


def kernel(
    shape,
    rhs_h, basis_h, trans_h, coup_h, csrc_h, near_h, nsrc_h, top_h, cc_h,
    out_ref,
    rhs_v, basis_v, trans_v, coup_v, csrc_s, near_v, nsrc_s, top_v, cc_v,
    wide_x, wide_c, slots, part, part_in,
    local_sem, halo_send, halo_recv, p_send, p_recv, r_send, r_recv,
):
    nx, ny, nz = shape
    count = nx * ny * nz
    leaves, rank, leaf = basis_v.shape
    rows = rhs_v.shape[0]
    slots_near = near_v.shape[1]
    slots_adm = coup_v.shape[1]
    topl = top_v.shape[0]
    gsize = 2**topl
    groups = count // gsize
    blocks = part.shape[1] // rank
    width = blocks * rank

    me = (lax.axis_index("gx") * ny + lax.axis_index("gy")) * nz + lax.axis_index("gz")
    group = me // gsize
    rel = me % gsize

    def place(e):
        return (e // (ny * nz), (e // nz) % ny, e % nz)

    loads = []
    for i, (src, dst) in enumerate(
        (
            (rhs_h, rhs_v), (basis_h, basis_v), (trans_h, trans_v), (top_h, top_v),
            (cc_h, cc_v), (csrc_h, csrc_s), (nsrc_h, nsrc_s), (coup_h, coup_v),
            (near_h, near_v),
        )
    ):
        load = pltpu.make_async_copy(src, dst, local_sem.at[i])
        load.start()
        loads.append(load)
    (l_rhs, l_basis, l_trans, l_top, l_cc, l_csrc, l_nsrc, l_coup, l_near) = loads

    if groups == 2:
        across = (((me + gsize) % count, None, 0),)
    else:
        across = ((me - gsize, group > 0, 1), (me + gsize, group < groups - 1, 0))
    has_prev, has_next = me > 0, me < count - 1

    barrier = pltpu.get_barrier_semaphore()

    def greet(e):
        pl.semaphore_signal(barrier, inc=1, device_id=place(e), device_id_type=MESH)

    def when(cond, fn):
        if cond is None:
            fn()
        else:
            pl.when(cond)(fn)

    peers = [group * gsize + (rel + r) % gsize for r in range(1, gsize)]
    for e in peers:
        greet(e)
    expected = jnp.int32(gsize - 1)
    out_prev = has_prev & (rel == 0)
    out_next = has_next & (rel == gsize - 1)
    for e, ok, _ in across:
        when(ok, functools.partial(greet, e))
        expected += 1 if ok is None else ok.astype(jnp.int32)
    for e, ok in ((me - 1, out_prev), (me + 1, out_next)):
        when(ok, functools.partial(greet, e))
        expected += ok.astype(jnp.int32)

    wide_x[leaves + 2 * REACH] = jnp.zeros((rows, leaf), BF16)
    wide_c[leaves + 2 * REACH] = jnp.zeros((rows, 2 * rank), BF16)
    low = lax.broadcasted_iota(jnp.int32, (rows, 2 * rank), 1) < rank

    l_rhs.wait()
    l_basis.wait()
    coeffs = []
    for t in range(leaves):
        block = rhs_v[:, t * leaf:(t + 1) * leaf]
        wide_x[REACH + t] = block
        basis = basis_v[t]
        both = mm_nt(block, jnp.concatenate([basis, basis], 0)).astype(BF16)
        wide_c[REACH + t] = both
        coeffs.append(both)
    pairs = [jnp.where(low, coeffs[t], coeffs[t + 1]) for t in range(0, leaves, 2)]
    l_trans.wait()
    root = mm(jnp.concatenate(pairs, 1), trans_v[...].reshape(leaves * rank, rank)).astype(BF16)
    slots[rel] = jnp.concatenate([root, root], 1)

    pl.semaphore_wait(barrier, expected)

    sends = []
    for e in peers:
        copy = pltpu.make_async_remote_copy(
            src_ref=slots.at[rel], dst_ref=slots.at[rel],
            send_sem=p_send.at[0], recv_sem=p_recv.at[0],
            device_id=place(e), device_id_type=MESH,
        )
        copy.start()

    def halo(buf, i, up):
        first, land = (leaves, 0) if up else (REACH, leaves + REACH)
        return pltpu.make_async_remote_copy(
            src_ref=buf.at[pl.ds(first, REACH)], dst_ref=buf.at[pl.ds(land, REACH)],
            send_sem=halo_send.at[i], recv_sem=halo_recv.at[i],
            device_id=place(me + 1 if up else me - 1), device_id_type=MESH,
        )

    ups = (halo(wide_c, 0, True), halo(wide_x, 1, True))
    downs = (halo(wide_c, 2, False), halo(wide_x, 3, False))

    @pl.when(has_next)
    def _():
        for copy in ups:
            copy.start()

    @pl.when(has_prev)
    def _():
        for copy in downs:
            copy.start()

    l_top.wait()
    l_cc.wait()
    lane_block = lax.broadcasted_iota(jnp.int32, (1, width), 1) // rank
    if groups == 2:
        dest = jnp.where(lane_block == 0, me, (me + gsize) % count)
    else:
        dest = jnp.where(lane_block == 0, me, jnp.where(lane_block == 1, me - gsize, me + gsize))
        dest = jnp.where(lane_block == 3, -8 * gsize, dest)
    row = lax.broadcasted_iota(jnp.int32, (rank, rank), 0)
    col = lax.broadcasted_iota(jnp.int32, (rank, rank), 1)
    down = jnp.where(row == col, 1.0, 0.0).astype(BF16)
    reach_mats = []
    for h in range(topl + 1):
        if h == 1:
            down = top_v[0, rel % 2]
        elif h > 1:
            down = mm(down, top_v[h - 1, (rel // 2 ** (h - 1)) % 2]).astype(BF16)
        reach_mats.append(
            mm_nt(cc_v[h].reshape(2 * rank, rank), jnp.concatenate([down] * blocks, 0))
        )

    def coupled(h, cluster):
        home = dest >> h
        return jnp.where(cluster == home - 1, reach_mats[h][:rank], 0.0) + jnp.where(
            cluster == home + 1, reach_mats[h][rank:], 0.0
        )

    level = [coupled(topl, group)]
    for h in range(topl - 1, -1, -1):
        wide = jnp.concatenate([m.astype(BF16) for m in level], 1)
        grown = mm(top_v[h].reshape(2 * rank, rank), wide)
        first = group * 2 ** (topl - h)
        level = [
            grown[(c % 2) * rank:(c % 2 + 1) * rank, (c // 2) * width:(c // 2 + 1) * width]
            + coupled(h, first + c)
            for c in range(2 ** (topl - h))
        ]
    gather_mat = jnp.concatenate([m.astype(BF16) for m in level], 0)

    spread = [mm_tn(trans_v[t], basis_v[t]).astype(BF16) for t in range(leaves)]
    spread = jnp.concatenate(spread, 1)
    spread = jnp.concatenate([spread] * blocks, 0)

    everyone = pltpu.make_async_copy(
        slots.at[pl.ds(0, gsize - 1)], slots.at[pl.ds(0, gsize - 1)], p_recv.at[0]
    )
    everyone.wait()
    held = [jnp.where(low, slots[c], slots[c + 1]) for c in range(0, gsize, 2)]
    own = mm(jnp.concatenate(held, 1), gather_mat)
    part[...] = own

    def partner(i, e, slot):
        return pltpu.make_async_remote_copy(
            src_ref=part, dst_ref=part_in.at[slot],
            send_sem=r_send.at[i], recv_sem=r_recv.at[slot],
            device_id=place(e), device_id_type=MESH,
        )

    partners = [(partner(i, e, slot), ok) for i, (e, ok, slot) in enumerate(across)]
    for copy, ok in partners:
        when(ok, copy.start)

    l_csrc.wait()
    l_nsrc.wait()
    l_coup.wait()
    l_near.wait()

    @pl.when(has_prev)
    def _():
        for copy in ups:
            copy.wait_recv()

    @pl.when(has_next)
    def _():
        for copy in downs:
            copy.wait_recv()

    anchor = me * leaves - REACH
    last = leaves + 2 * REACH

    def spot(source):
        return jnp.where(source >= 0, jnp.clip(source - anchor, 0, last - 1), last)

    sums = []
    for t in range(leaves):
        picked = [wide_c[spot(csrc_s[t, a])] for a in range(slots_adm)]
        picked = [jnp.where(low, picked[a], picked[a + 1]) for a in range(0, slots_adm, 2)]
        field = mm(
            jnp.concatenate(picked, 1), coup_v[t].reshape(slots_adm * rank, rank)
        ).astype(BF16)
        inputs = [wide_x[REACH + t]]
        inputs += [wide_x[spot(nsrc_s[t, n])] for n in range(1, slots_near)]
        sums.append(
            mm(jnp.concatenate(inputs, 1), near_v[t].reshape(slots_near * leaf, leaf))
            + mm(field, basis_v[t])
        )

    cells = lax.broadcasted_iota(jnp.int32, (rows, width), 1) // rank
    if groups == 2:
        partners[0][0].wait_recv()
        total = jnp.where(cells == 0, own, part_in[0])
    else:
        def arrived(slot, ok):
            pltpu.make_async_copy(part_in.at[slot], part_in.at[slot], r_recv.at[slot]).wait()

        pl.when(group > 0)(functools.partial(arrived, 0, None))
        pl.when(group < groups - 1)(functools.partial(arrived, 1, None))
        total = jnp.where(cells == 0, own, 0.0)
        total = jnp.where((cells == 1) & (group < groups - 1), part_in[1], total)
        total = jnp.where((cells == 2) & (group > 0), part_in[0], total)
    far = mm(total.astype(BF16), spread)
    for t in range(leaves):
        out_ref[:, t * leaf:(t + 1) * leaf] = (
            sums[t] + far[:, t * leaf:(t + 1) * leaf]
        ).astype(BF16)

    pltpu.make_async_copy(
        slots.at[pl.ds(0, gsize - 1)], slots.at[pl.ds(0, gsize - 1)], p_send.at[0]
    ).wait()
    for copy, ok in partners:
        when(ok, copy.wait_send)

    @pl.when(has_next)
    def _():
        for copy in ups:
            copy.wait_send()

    @pl.when(has_prev)
    def _():
        for copy in downs:
            copy.wait_send()


def solution(mesh):
    shape = tuple(mesh.shape[a] for a in AXES)
    count = shape[0] * shape[1] * shape[2]

    def local(rhs, basis, trans, coup, csrc, near, nsrc, top, cc):
        leaves, rank, leaf = basis.shape
        rows = rhs.shape[0]
        gsize = 2 ** top.shape[0]
        blocks = 2 if count == 2 * gsize else 4
        args = (rhs, basis, trans, coup, csrc, near, nsrc, top, cc)

        def room(x):
            kind = pltpu.SMEM if x.dtype == jnp.int32 else pltpu.VMEM
            return kind(x.shape, x.dtype)

        dma = pltpu.SemaphoreType.DMA
        return pl.pallas_call(
            functools.partial(kernel, shape),
            out_shape=jax.ShapeDtypeStruct(rhs.shape, BF16),
            in_specs=[pl.BlockSpec(memory_space=pl.ANY)] * len(args),
            out_specs=pl.BlockSpec(memory_space=pltpu.VMEM),
            scratch_shapes=[room(x) for x in args] + [
                pltpu.VMEM((leaves + 2 * REACH + 1, rows, leaf), BF16),
                pltpu.VMEM((leaves + 2 * REACH + 1, rows, 2 * rank), BF16),
                pltpu.VMEM((gsize, rows, 2 * rank), BF16),
                pltpu.VMEM((rows, blocks * rank), F32),
                pltpu.VMEM((blocks // 2, rows, blocks * rank), F32),
                dma((len(args),)), dma((4,)), dma((4,)), dma((1,)), dma((1,)),
                dma((2,)), dma((2,)),
            ],
            compiler_params=pltpu.CompilerParams(collective_id=0, has_side_effects=True),
        )(*args)

    placed = (
        P(None, AXES),
        P(AXES, None, None),
        P(AXES, None, None),
        P(AXES, None, None, None),
        P(AXES, None),
        P(AXES, None, None, None),
        P(AXES, None),
        P(),
        P(),
    )
    return jax.shard_map(
        local, mesh=mesh, in_specs=placed, out_specs=P(None, AXES), check_vma=False
    )
```

```python
import functools

import jax
import jax.numpy as jnp
from jax import lax
from jax.experimental import pallas as pl
from jax.experimental.pallas import tpu as pltpu
from jax.sharding import PartitionSpec as P

AXES = ("gx", "gy", "gz")
REACH = 2
MESH = pl.DeviceIdType.MESH
BF16 = jnp.bfloat16
F32 = jnp.float32


def mm(a, b):
    return jnp.dot(a, b, preferred_element_type=F32)


def mm_nt(a, b):
    return lax.dot_general(a, b, (((1,), (1,)), ((), ())), preferred_element_type=F32)


def mm_tn(a, b):
    return lax.dot_general(a, b, (((0,), (0,)), ((), ())), preferred_element_type=F32)


def kernel(
    shape,
    rhs_h, basis_h, trans_h, coup_h, csrc_h, near_h, nsrc_h, top_h, cc_h,
    out_ref,
    rhs_v, basis_v, trans_v, coup_v, csrc_s, near_v, nsrc_s, top_v, cc_v,
    wide_x, wide_c, slots,
    local_sem, halo_send, halo_recv, p_send, p_recv,
):
    nx, ny, nz = shape
    count = nx * ny * nz
    leaves, rank, leaf = basis_v.shape
    rows = rhs_v.shape[0]
    slots_near = near_v.shape[1]
    slots_adm = coup_v.shape[1]
    topl = top_v.shape[0]
    gsize = 2**topl
    groups = count // gsize
    blocks = 2 if groups == 2 else 4
    width = blocks * rank

    me = (lax.axis_index("gx") * ny + lax.axis_index("gy")) * nz + lax.axis_index("gz")
    group = me // gsize
    rel = me % gsize

    def place(e):
        return (e // (ny * nz), (e // nz) % ny, e % nz)

    loads = []
    for i, (src, dst) in enumerate(
        (
            (rhs_h, rhs_v), (basis_h, basis_v), (trans_h, trans_v), (top_h, top_v),
            (cc_h, cc_v), (csrc_h, csrc_s), (nsrc_h, nsrc_s), (coup_h, coup_v),
            (near_h, near_v),
        )
    ):
        load = pltpu.make_async_copy(src, dst, local_sem.at[i])
        load.start()
        loads.append(load)
    (l_rhs, l_basis, l_trans, l_top, l_cc, l_csrc, l_nsrc, l_coup, l_near) = loads

    if groups == 2:
        mine = group
        across = ((1 - group, None, 1 - group, group),)
    else:
        mine = 1
        across = ((group - 1, group > 0, 0, 2), (group + 1, group < groups - 1, 2, 0))
    has_prev, has_next = me > 0, me < count - 1

    def when(cond, fn):
        if cond is None:
            fn()
        else:
            pl.when(cond)(fn)

    far_first = sorted(range(gsize), key=lambda r: -(r % nz))

    def each_peer(fn):
        for i, (g, ok, _, there) in enumerate(across):
            def outer(i=i, g=g, there=there):
                for r in far_first:
                    fn(g * gsize + (rel ^ r), there, i + 1)
            when(ok, outer)
        for r in far_first:
            if r:
                fn(group * gsize + (rel ^ r), mine, 0)

    barrier = pltpu.get_barrier_semaphore()
    each_peer(
        lambda e, there, i: pl.semaphore_signal(
            barrier, inc=1, device_id=place(e), device_id_type=MESH
        )
    )
    expected = jnp.int32(gsize - 1)
    for _, ok, _, _ in across:
        expected += gsize if ok is None else gsize * ok.astype(jnp.int32)

    wide_x[leaves + 2 * REACH] = jnp.zeros((rows, leaf), BF16)
    wide_c[leaves + 2 * REACH] = jnp.zeros((rows, 2 * rank), BF16)
    low = lax.broadcasted_iota(jnp.int32, (rows, 2 * rank), 1) < rank

    l_rhs.wait()
    l_basis.wait()
    coeffs = []
    for t in range(leaves):
        block = rhs_v[:, t * leaf:(t + 1) * leaf]
        wide_x[REACH + t] = block
        basis = basis_v[t]
        both = mm_nt(block, jnp.concatenate([basis, basis], 0)).astype(BF16)
        wide_c[REACH + t] = both
        coeffs.append(both)
    pairs = [jnp.where(low, coeffs[t], coeffs[t + 1]) for t in range(0, leaves, 2)]
    l_trans.wait()
    root = mm(jnp.concatenate(pairs, 1), trans_v[...].reshape(leaves * rank, rank)).astype(BF16)
    slots[mine, rel] = jnp.concatenate([root, root], 1)

    pl.semaphore_wait(barrier, expected)

    each_peer(
        lambda e, there, i: pltpu.make_async_remote_copy(
            src_ref=slots.at[mine, rel], dst_ref=slots.at[there, rel],
            send_sem=p_send.at[i], recv_sem=p_recv.at[there],
            device_id=place(e), device_id_type=MESH,
        ).start()
    )

    def halo(buf, i, up):
        first, land = (leaves, 0) if up else (REACH, leaves + REACH)
        return pltpu.make_async_remote_copy(
            src_ref=buf.at[pl.ds(first, REACH)], dst_ref=buf.at[pl.ds(land, REACH)],
            send_sem=halo_send.at[i], recv_sem=halo_recv.at[i],
            device_id=place(me + 1 if up else me - 1), device_id_type=MESH,
        )

    ups = (halo(wide_c, 0, True), halo(wide_x, 1, True))
    downs = (halo(wide_c, 2, False), halo(wide_x, 3, False))

    @pl.when(has_next)
    def _():
        for copy in ups:
            copy.start()

    @pl.when(has_prev)
    def _():
        for copy in downs:
            copy.start()

    l_top.wait()
    l_cc.wait()
    lane_block = lax.broadcasted_iota(jnp.int32, (1, width), 1) // rank
    if groups == 2:
        lane_group = lane_block
    else:
        lane_group = jnp.where(lane_block < 3, group - 1 + lane_block, -8)
    row = lax.broadcasted_iota(jnp.int32, (rank, rank), 0)
    col = lax.broadcasted_iota(jnp.int32, (rank, rank), 1)
    down = jnp.where(row == col, 1.0, 0.0).astype(BF16)
    reach_mats = []
    for h in range(topl + 1):
        if h == 1:
            down = top_v[0, rel % 2]
        elif h > 1:
            down = mm(down, top_v[h - 1, (rel // 2 ** (h - 1)) % 2]).astype(BF16)
        reach_mats.append(
            mm_nt(cc_v[h].reshape(2 * rank, rank), jnp.concatenate([down] * blocks, 0))
        )

    def coupled(h, c):
        cluster = lane_group * 2 ** (topl - h) + c
        home = me // 2**h
        return jnp.where(cluster == home - 1, reach_mats[h][:rank], 0.0) + jnp.where(
            cluster == home + 1, reach_mats[h][rank:], 0.0
        )

    level = [coupled(topl, 0)]
    for h in range(topl - 1, -1, -1):
        wide = jnp.concatenate([m.astype(BF16) for m in level], 1)
        grown = mm(top_v[h].reshape(2 * rank, rank), wide)
        level = [
            grown[(c % 2) * rank:(c % 2 + 1) * rank, (c // 2) * width:(c // 2 + 1) * width]
            + coupled(h, c)
            for c in range(2 ** (topl - h))
        ]
    gather_mat = jnp.concatenate([m.astype(BF16) for m in level], 0)

    spread = [mm_tn(trans_v[t], basis_v[t]).astype(BF16) for t in range(leaves)]
    spread = jnp.concatenate(spread, 1)
    spread = jnp.concatenate([spread] * blocks, 0)

    l_csrc.wait()
    l_nsrc.wait()
    l_coup.wait()
    l_near.wait()

    @pl.when(has_prev)
    def _():
        for copy in ups:
            copy.wait_recv()

    @pl.when(has_next)
    def _():
        for copy in downs:
            copy.wait_recv()

    anchor = me * leaves - REACH
    last = leaves + 2 * REACH

    def spot(source):
        return jnp.where(source >= 0, jnp.clip(source - anchor, 0, last - 1), last)

    sums = []
    for t in range(leaves):
        picked = [wide_c[spot(csrc_s[t, a])] for a in range(slots_adm)]
        picked = [jnp.where(low, picked[a], picked[a + 1]) for a in range(0, slots_adm, 2)]
        field = mm(
            jnp.concatenate(picked, 1), coup_v[t].reshape(slots_adm * rank, rank)
        ).astype(BF16)
        inputs = [wide_x[REACH + t]]
        inputs += [wide_x[spot(nsrc_s[t, n])] for n in range(1, slots_near)]
        sums.append(
            mm(jnp.concatenate(inputs, 1), near_v[t].reshape(slots_near * leaf, leaf))
            + mm(field, basis_v[t])
        )

    def landed(block, number, sem):
        group_slots = slots.at[block, pl.ds(0, number)]
        pltpu.make_async_copy(group_slots, group_slots, sem).wait()

    landed(mine, gsize - 1, p_recv.at[mine])
    for _, ok, here, _ in across:
        when(ok, functools.partial(landed, here, gsize, p_recv.at[here]))
    used = 2 if groups == 2 else 3
    held = [
        jnp.concatenate(
            [jnp.where(low, slots[b, c], slots[b, c + 1]) for c in range(0, gsize, 2)], 1
        )
        for b in range(used)
    ]
    fields = mm(jnp.concatenate(held, 0), gather_mat)
    cells = lax.broadcasted_iota(jnp.int32, (rows, width), 1) // rank
    total = jnp.zeros((rows, width), F32)
    for b in range(used):
        ours = cells == b
        if groups != 2 and b != 1:
            ours = ours & (group > 0 if b == 0 else group < groups - 1)
        total = jnp.where(ours, fields[b * rows:(b + 1) * rows], total)
    far = mm(total.astype(BF16), spread)
    for t in range(leaves):
        out_ref[:, t * leaf:(t + 1) * leaf] = (
            sums[t] + far[:, t * leaf:(t + 1) * leaf]
        ).astype(BF16)

    landed(mine, gsize - 1, p_send.at[0])
    for i, (_, ok, here, _) in enumerate(across):
        when(ok, functools.partial(landed, here, gsize, p_send.at[i + 1]))

    @pl.when(has_next)
    def _():
        for copy in ups:
            copy.wait_send()

    @pl.when(has_prev)
    def _():
        for copy in downs:
            copy.wait_send()


def solution(mesh):
    shape = tuple(mesh.shape[a] for a in AXES)
    count = shape[0] * shape[1] * shape[2]

    def local(rhs, basis, trans, coup, csrc, near, nsrc, top, cc):
        leaves, rank, leaf = basis.shape
        rows = rhs.shape[0]
        gsize = 2 ** top.shape[0]
        blocks = 2 if count == 2 * gsize else 4
        args = (rhs, basis, trans, coup, csrc, near, nsrc, top, cc)

        def room(x):
            kind = pltpu.SMEM if x.dtype == jnp.int32 else pltpu.VMEM
            return kind(x.shape, x.dtype)

        dma = pltpu.SemaphoreType.DMA
        return pl.pallas_call(
            functools.partial(kernel, shape),
            out_shape=pltpu.VMEM(rhs.shape, BF16),
            in_specs=[pl.BlockSpec(memory_space=pl.ANY)] * len(args),
            out_specs=pl.BlockSpec(memory_space=pltpu.VMEM),
            scratch_shapes=[room(x) for x in args] + [
                pltpu.VMEM((leaves + 2 * REACH + 1, rows, leaf), BF16),
                pltpu.VMEM((leaves + 2 * REACH + 1, rows, 2 * rank), BF16),
                pltpu.VMEM((blocks, gsize, rows, 2 * rank), BF16),
                dma((len(args),)), dma((4,)), dma((4,)), dma((3,)), dma((blocks,)),
            ],
            compiler_params=pltpu.CompilerParams(collective_id=0, has_side_effects=True),
        )(*(pltpu.with_memory_space_constraint(x, pltpu.HBM) for x in args))

    placed = (
        P(None, AXES),
        P(AXES, None, None),
        P(AXES, None, None),
        P(AXES, None, None, None),
        P(AXES, None),
        P(AXES, None, None, None),
        P(AXES, None),
        P(),
        P(),
    )
    return jax.shard_map(
        local, mesh=mesh, in_specs=placed, out_specs=P(None, AXES), check_vma=False
    )
```

```python
import functools

import jax
import jax.numpy as jnp
from jax import lax
from jax.experimental import pallas as pl
from jax.experimental.pallas import tpu as pltpu
from jax.sharding import PartitionSpec as P

AXES = ("gx", "gy", "gz")
REACH = 2
LOW = 2
MESH = pl.DeviceIdType.MESH
BF16 = jnp.bfloat16
F32 = jnp.float32


def mm(a, b):
    return jnp.dot(a, b, preferred_element_type=F32)


def mm_nt(a, b):
    return lax.dot_general(a, b, (((1,), (1,)), ((), ())), preferred_element_type=F32)


def mm_tn(a, b):
    return lax.dot_general(a, b, (((0,), (0,)), ((), ())), preferred_element_type=F32)


def kernel(
    shape,
    rhs_h, basis_h, trans_h, coup_h, csrc_h, near_h, nsrc_h, top_h, cc_h,
    out_ref,
    rhs_v, basis_v, trans_v, coup_v, csrc_s, near_v, nsrc_s, top_v, cc_v,
    wide_x, wide_c, slots, part, part_in,
    local_sem, halo_send, halo_recv, p_send, p_recv, r_send, r_recv,
):
    nx, ny, nz = shape
    count = nx * ny * nz
    leaves, rank, leaf = basis_v.shape
    rows = rhs_v.shape[0]
    slots_near = near_v.shape[1]
    slots_adm = coup_v.shape[1]
    topl = top_v.shape[0]
    gsize = 2**topl
    groups = count // gsize
    line = 2**LOW
    lines = gsize // line
    width = part.shape[0] * 2 * rank

    me = (lax.axis_index("gx") * ny + lax.axis_index("gy")) * nz + lax.axis_index("gz")
    group = me // gsize
    mine_line = me // line
    rel = me % line
    own = mine_line % lines

    def place(e):
        return (e // (ny * nz), (e // nz) % ny, e % nz)

    loads = []
    for i, (src, dst) in enumerate(
        (
            (rhs_h, rhs_v), (basis_h, basis_v), (trans_h, trans_v), (top_h, top_v),
            (cc_h, cc_v), (csrc_h, csrc_s), (nsrc_h, nsrc_s), (coup_h, coup_v),
            (near_h, near_v),
        )
    ):
        load = pltpu.make_async_copy(src, dst, local_sem.at[i])
        load.start()
        loads.append(load)
    (l_rhs, l_basis, l_trans, l_top, l_cc, l_csrc, l_nsrc, l_coup, l_near) = loads

    if groups == 2:
        mine = group
        across = ((1 - group, None, 1 - group, group),)
    else:
        mine = 1
        across = ((group - 1, group > 0, 0, 2), (group + 1, group < groups - 1, 2, 0))
    has_prev, has_next = me > 0, me < count - 1

    def when(cond, fn):
        if cond is None:
            fn()
        else:
            pl.when(cond)(fn)

    mates = [mine_line * line + (rel ^ r) for r in range(line - 1, 0, -1)]

    def each_line(fn):
        for i, (g, ok, here, there) in enumerate(across):
            def outer(i=i, g=g, here=here, there=there):
                for k in range(lines):
                    l = own ^ k
                    fn(g * gsize + l * line + rel, here, l, there, i + 1)
            when(ok, outer)
        for k in range(lines - 1, 0, -1):
            l = own ^ k
            fn(group * gsize + l * line + rel, mine, l, mine, 0)

    barrier = pltpu.get_barrier_semaphore()

    def greet(e, *_):
        pl.semaphore_signal(barrier, inc=1, device_id=place(e), device_id_type=MESH)

    for e in mates:
        greet(e)
    out_prev = has_prev & (rel == 0)
    out_next = has_next & (rel == line - 1)
    when(out_prev, functools.partial(greet, me - 1))
    when(out_next, functools.partial(greet, me + 1))
    each_line(greet)
    expected = jnp.int32(line - 1 + lines - 1)
    expected += out_prev.astype(jnp.int32) + out_next.astype(jnp.int32)
    for _, ok, _, _ in across:
        expected += lines if ok is None else lines * ok.astype(jnp.int32)

    wide_x[leaves + 2 * REACH] = jnp.zeros((rows, leaf), BF16)
    wide_c[leaves + 2 * REACH] = jnp.zeros((rows, 2 * rank), BF16)
    low = lax.broadcasted_iota(jnp.int32, (rows, 2 * rank), 1) < rank

    l_rhs.wait()
    l_basis.wait()
    coeffs = []
    for t in range(leaves):
        block = rhs_v[:, t * leaf:(t + 1) * leaf]
        wide_x[REACH + t] = block
        basis = basis_v[t]
        both = mm_nt(block, jnp.concatenate([basis, basis], 0)).astype(BF16)
        wide_c[REACH + t] = both
        coeffs.append(both)
    pairs = [jnp.where(low, coeffs[t], coeffs[t + 1]) for t in range(0, leaves, 2)]
    l_trans.wait()
    root = mm(jnp.concatenate(pairs, 1), trans_v[...].reshape(leaves * rank, rank)).astype(BF16)
    slots[rel] = jnp.concatenate([root, root], 1)

    pl.semaphore_wait(barrier, expected)

    for e in mates:
        pltpu.make_async_remote_copy(
            src_ref=slots.at[rel], dst_ref=slots.at[rel],
            send_sem=p_send.at[0], recv_sem=p_recv.at[0],
            device_id=place(e), device_id_type=MESH,
        ).start()

    def halo(buf, i, up):
        first, land = (leaves, 0) if up else (REACH, leaves + REACH)
        return pltpu.make_async_remote_copy(
            src_ref=buf.at[pl.ds(first, REACH)], dst_ref=buf.at[pl.ds(land, REACH)],
            send_sem=halo_send.at[i], recv_sem=halo_recv.at[i],
            device_id=place(me + 1 if up else me - 1), device_id_type=MESH,
        )

    ups = (halo(wide_c, 0, True), halo(wide_x, 1, True))
    downs = (halo(wide_c, 2, False), halo(wide_x, 3, False))

    @pl.when(has_next)
    def _():
        for copy in ups:
            copy.start()

    @pl.when(has_prev)
    def _():
        for copy in downs:
            copy.start()

    l_top.wait()
    l_cc.wait()
    lane_block = lax.broadcasted_iota(jnp.int32, (1, width), 1) // rank
    lane_group = lane_block // lines
    if groups != 2:
        lane_group = lane_group + (group - 1)
    dest = lane_group * gsize + (lane_block % lines) * line + rel
    row = lax.broadcasted_iota(jnp.int32, (rank, rank), 0)
    col = lax.broadcasted_iota(jnp.int32, (rank, rank), 1)
    down = jnp.where(row == col, 1.0, 0.0).astype(BF16)
    reach_mats = []
    for h in range(topl + 1):
        if h == 1:
            down = top_v[0, rel % 2]
        elif 1 < h <= LOW:
            down = mm(down, top_v[h - 1, (rel // 2 ** (h - 1)) % 2]).astype(BF16)
        elif h > LOW:
            down = jnp.concatenate([mm(down, top_v[h - 1, p]) for p in range(2)], 0).astype(BF16)
        stack = down if h > LOW else jnp.concatenate([down, down], 0)
        mat = mm_nt(cc_v[h].reshape(2 * rank, rank), stack)
        reach_mats.append(jnp.concatenate([mat] * (width // mat.shape[1]), 1))

    def coupled(h, cluster):
        home = dest >> h
        return jnp.where(cluster == home - 1, reach_mats[h][:rank], 0.0) + jnp.where(
            cluster == home + 1, reach_mats[h][rank:], 0.0
        )

    level = [coupled(topl, group)]
    for h in range(topl - 1, -1, -1):
        wide = jnp.concatenate([m.astype(BF16) for m in level], 1)
        if h >= LOW:
            level = [mm(top_v[h, (me >> h) % 2], wide) + coupled(h, me >> h)]
            continue
        grown = mm(top_v[h].reshape(2 * rank, rank), wide)
        level = [
            grown[(c % 2) * rank:(c % 2 + 1) * rank, (c // 2) * width:(c // 2 + 1) * width]
            + coupled(h, mine_line * 2 ** (LOW - h) + c)
            for c in range(2 ** (LOW - h))
        ]
    gather_mat = jnp.concatenate([m.astype(BF16) for m in level], 0)

    spread = [mm_tn(trans_v[t], basis_v[t]).astype(BF16) for t in range(leaves)]
    spread = jnp.concatenate(spread, 1)
    spread = jnp.concatenate([spread, spread], 0)

    def landed(buf, number, sem):
        some = buf.at[pl.ds(0, number)]
        pltpu.make_async_copy(some, some, sem).wait()

    landed(slots, line - 1, p_recv.at[0])
    held = [jnp.where(low, slots[c], slots[c + 1]) for c in range(0, line, 2)]
    parts = mm(jnp.concatenate(held, 1), gather_mat)
    for i in range(part.shape[0]):
        part[i] = parts[:, i * 2 * rank:(i + 1) * 2 * rank]
    each_line(
        lambda e, here, l, there, i: pltpu.make_async_remote_copy(
            src_ref=part.at[here * (lines // 2) + l // 2], dst_ref=part_in.at[there * lines + own],
            send_sem=r_send.at[i], recv_sem=r_recv.at[there],
            device_id=place(e), device_id_type=MESH,
        ).start()
    )
    part_in[mine * lines + own] = part[mine * (lines // 2) + own // 2]

    l_csrc.wait()
    l_nsrc.wait()
    l_coup.wait()
    l_near.wait()

    @pl.when(has_prev)
    def _():
        for copy in ups:
            copy.wait_recv()

    @pl.when(has_next)
    def _():
        for copy in downs:
            copy.wait_recv()

    anchor = me * leaves - REACH
    last = leaves + 2 * REACH

    def spot(source):
        return jnp.where(source >= 0, jnp.clip(source - anchor, 0, last - 1), last)

    sums = []
    for t in range(leaves):
        picked = [wide_c[spot(csrc_s[t, a])] for a in range(slots_adm)]
        picked = [jnp.where(low, picked[a], picked[a + 1]) for a in range(0, slots_adm, 2)]
        field = mm(
            jnp.concatenate(picked, 1), coup_v[t].reshape(slots_adm * rank, rank)
        ).astype(BF16)
        inputs = [wide_x[REACH + t]]
        inputs += [wide_x[spot(nsrc_s[t, n])] for n in range(1, slots_near)]
        sums.append(
            mm(jnp.concatenate(inputs, 1), near_v[t].reshape(slots_near * leaf, leaf))
            + mm(field, basis_v[t])
        )

    landed(part_in, lines - 1, r_recv.at[mine])
    for _, ok, here, _ in across:
        when(ok, functools.partial(landed, part_in, lines, r_recv.at[here]))
    total = jnp.zeros((rows, 2 * rank), F32)
    for j in range(part_in.shape[0]):
        term = part_in[j]
        if groups != 2 and j // lines != 1:
            term = jnp.where(group > 0 if j < lines else group < groups - 1, term, 0.0)
        total += term
    total = jnp.where(low == (own % 2 == 0), total, 0.0)
    far = mm(total.astype(BF16), spread)
    for t in range(leaves):
        out_ref[:, t * leaf:(t + 1) * leaf] = (
            sums[t] + far[:, t * leaf:(t + 1) * leaf]
        ).astype(BF16)

    landed(slots, line - 1, p_send.at[0])
    landed(part_in, lines - 1, r_send.at[0])
    for i, (_, ok, _, _) in enumerate(across):
        when(ok, functools.partial(landed, part_in, lines, r_send.at[i + 1]))

    @pl.when(has_next)
    def _():
        for copy in ups:
            copy.wait_send()

    @pl.when(has_prev)
    def _():
        for copy in downs:
            copy.wait_send()


def solution(mesh):
    shape = tuple(mesh.shape[a] for a in AXES)
    count = shape[0] * shape[1] * shape[2]

    def local(rhs, basis, trans, coup, csrc, near, nsrc, top, cc):
        leaves, rank, leaf = basis.shape
        rows = rhs.shape[0]
        gsize = 2 ** top.shape[0]
        lines = (2 if count == 2 * gsize else 3) * gsize // 2**LOW
        args = (rhs, basis, trans, coup, csrc, near, nsrc, top, cc)

        def room(x):
            kind = pltpu.SMEM if x.dtype == jnp.int32 else pltpu.VMEM
            return kind(x.shape, x.dtype)

        dma = pltpu.SemaphoreType.DMA
        return pl.pallas_call(
            functools.partial(kernel, shape),
            out_shape=pltpu.VMEM(rhs.shape, BF16),
            in_specs=[pl.BlockSpec(memory_space=pl.ANY)] * len(args),
            out_specs=pl.BlockSpec(memory_space=pltpu.VMEM),
            scratch_shapes=[room(x) for x in args] + [
                pltpu.VMEM((leaves + 2 * REACH + 1, rows, leaf), BF16),
                pltpu.VMEM((leaves + 2 * REACH + 1, rows, 2 * rank), BF16),
                pltpu.VMEM((2**LOW, rows, 2 * rank), BF16),
                pltpu.VMEM((lines // 2, rows, 2 * rank), F32),
                pltpu.VMEM((lines, rows, 2 * rank), F32),
                dma((len(args),)), dma((4,)), dma((4,)), dma((1,)), dma((1,)),
                dma((3,)), dma((3,)),
            ],
            compiler_params=pltpu.CompilerParams(collective_id=0, has_side_effects=True),
        )(*(pltpu.with_memory_space_constraint(x, pltpu.HBM) for x in args))

    placed = (
        P(None, AXES),
        P(AXES, None, None),
        P(AXES, None, None),
        P(AXES, None, None, None),
        P(AXES, None),
        P(AXES, None, None, None),
        P(AXES, None),
        P(),
        P(),
    )
    return jax.shard_map(
        local, mesh=mesh, in_specs=placed, out_specs=P(None, AXES), check_vma=False
    )
```

```python
import functools

import jax
import jax.numpy as jnp
from jax import lax
from jax.experimental import pallas as pl
from jax.experimental.pallas import tpu as pltpu
from jax.sharding import PartitionSpec as P

AXES = ("gx", "gy", "gz")
REACH = 2
LOW = 2
MESH = pl.DeviceIdType.MESH
BF16 = jnp.bfloat16
F32 = jnp.float32


def mm(a, b):
    return jnp.dot(a, b, preferred_element_type=F32)


def mm_nt(a, b):
    return lax.dot_general(a, b, (((1,), (1,)), ((), ())), preferred_element_type=F32)


def mm_tn(a, b):
    return lax.dot_general(a, b, (((0,), (0,)), ((), ())), preferred_element_type=F32)


def kernel(
    shape,
    rhs_h, basis_h, trans_h, coup_h, csrc_h, near_h, nsrc_h, top_h, cc_h,
    out_ref,
    rhs_v, basis_v, trans_v, coup_v, csrc_s, near_v, nsrc_s, top_v, cc_v,
    wide_x, wide_c, slots, part, part_in, gather_v, spread_v, first_v,
    local_sem, halo_send, halo_recv, p_send, p_recv, r_send, r_recv,
):
    nx, ny, nz = shape
    count = nx * ny * nz
    leaves, rank, leaf = basis_v.shape
    rows = rhs_v.shape[0]
    slots_near = near_v.shape[1]
    slots_adm = coup_v.shape[1]
    topl = top_v.shape[0]
    gsize = 2**topl
    groups = count // gsize
    line = 2**LOW
    lines = gsize // line
    width = part.shape[0] * 2 * rank

    me = (lax.axis_index("gx") * ny + lax.axis_index("gy")) * nz + lax.axis_index("gz")
    group = me // gsize
    mine_line = me // line
    rel = me % line
    own = mine_line % lines

    def place(e):
        return (e // (ny * nz), (e // nz) % ny, e % nz)

    loads = []
    for i, (src, dst) in enumerate(
        (
            (rhs_h, rhs_v), (basis_h, basis_v), (trans_h, trans_v), (top_h, top_v),
            (cc_h, cc_v), (csrc_h, csrc_s), (nsrc_h, nsrc_s), (coup_h, coup_v),
            (near_h, near_v),
        )
    ):
        load = pltpu.make_async_copy(src, dst, local_sem.at[i])
        load.start()
        loads.append(load)
    (l_rhs, l_basis, l_trans, l_top, l_cc, l_csrc, l_nsrc, l_coup, l_near) = loads

    if groups == 2:
        mine = group
        across = ((1 - group, None, 1 - group, group),)
    else:
        mine = 1
        across = ((group - 1, group > 0, 0, 2), (group + 1, group < groups - 1, 2, 0))
    has_prev, has_next = me > 0, me < count - 1

    def when(cond, fn):
        if cond is None:
            fn()
        else:
            pl.when(cond)(fn)

    mates = [mine_line * line + (rel ^ r) for r in range(line - 1, 0, -1)]

    def each_line(fn):
        for i, (g, ok, here, there) in enumerate(across):
            def outer(i=i, g=g, here=here, there=there):
                for k in range(lines):
                    l = own ^ k
                    fn(g * gsize + l * line + rel, here, l, there, i + 1)
            when(ok, outer)
        for k in range(lines - 1, 0, -1):
            l = own ^ k
            fn(group * gsize + l * line + rel, mine, l, mine, 0)

    barrier = pltpu.get_barrier_semaphore()

    def greet(e, *_):
        pl.semaphore_signal(barrier, inc=1, device_id=place(e), device_id_type=MESH)

    for e in mates:
        greet(e)
    out_prev = has_prev & (rel == 0)
    out_next = has_next & (rel == line - 1)
    when(out_prev, functools.partial(greet, me - 1))
    when(out_next, functools.partial(greet, me + 1))
    each_line(greet)
    expected = jnp.int32(line - 1 + lines - 1)
    expected += out_prev.astype(jnp.int32) + out_next.astype(jnp.int32)
    for _, ok, _, _ in across:
        expected += lines if ok is None else lines * ok.astype(jnp.int32)

    wide_x[leaves + 2 * REACH] = jnp.zeros((rows, leaf), BF16)
    wide_c[leaves + 2 * REACH] = jnp.zeros((rows, 2 * rank), BF16)
    low = lax.broadcasted_iota(jnp.int32, (rows, 2 * rank), 1) < rank

    l_rhs.wait()
    l_basis.wait()
    coeffs = []
    for t in range(leaves):
        block = rhs_v[:, t * leaf:(t + 1) * leaf]
        wide_x[REACH + t] = block
        basis = basis_v[t]
        both = mm_nt(block, jnp.concatenate([basis, basis], 0)).astype(BF16)
        wide_c[REACH + t] = both
        coeffs.append(both)
    pairs = [jnp.where(low, coeffs[t], coeffs[t + 1]) for t in range(0, leaves, 2)]
    l_trans.wait()
    root = mm(jnp.concatenate(pairs, 1), trans_v[...].reshape(leaves * rank, rank)).astype(BF16)
    slots[rel] = jnp.concatenate([root, root], 1)

    def halo(buf, i, up):
        first, land = (leaves, 0) if up else (REACH, leaves + REACH)
        return pltpu.make_async_remote_copy(
            src_ref=buf.at[pl.ds(first, REACH)], dst_ref=buf.at[pl.ds(land, REACH)],
            send_sem=halo_send.at[i], recv_sem=halo_recv.at[i],
            device_id=place(me + 1 if up else me - 1), device_id_type=MESH,
        )

    ups = (halo(wide_c, 0, True), halo(wide_x, 1, True))
    downs = (halo(wide_c, 2, False), halo(wide_x, 3, False))

    def send():
        pl.semaphore_wait(barrier, expected)

        for e in mates:
            pltpu.make_async_remote_copy(
                src_ref=slots.at[rel], dst_ref=slots.at[rel],
                send_sem=p_send.at[0], recv_sem=p_recv.at[0],
                device_id=place(e), device_id_type=MESH,
            ).start()
        @pl.when(has_next)
        def _():
            for copy in ups:
                copy.start()

        @pl.when(has_prev)
        def _():
            for copy in downs:
                copy.start()

    def prepare():
        l_top.wait()
        l_cc.wait()
        lane_block = lax.broadcasted_iota(jnp.int32, (1, width), 1) // rank
        lane_group = lane_block // lines
        if groups != 2:
            lane_group = lane_group + (group - 1)
        dest = lane_group * gsize + (lane_block % lines) * line + rel
        row = lax.broadcasted_iota(jnp.int32, (rank, rank), 0)
        col = lax.broadcasted_iota(jnp.int32, (rank, rank), 1)
        down = jnp.where(row == col, 1.0, 0.0).astype(BF16)
        reach_mats = []
        for h in range(topl + 1):
            if h == 1:
                down = top_v[0, rel % 2]
            elif 1 < h <= LOW:
                down = mm(down, top_v[h - 1, (rel // 2 ** (h - 1)) % 2]).astype(BF16)
            elif h > LOW:
                down = jnp.concatenate([mm(down, top_v[h - 1, p]) for p in range(2)], 0).astype(BF16)
            stack = down if h > LOW else jnp.concatenate([down, down], 0)
            mat = mm_nt(cc_v[h].reshape(2 * rank, rank), stack)
            reach_mats.append(jnp.concatenate([mat] * (width // mat.shape[1]), 1))

        def coupled(h, cluster):
            home = dest >> h
            return jnp.where(cluster == home - 1, reach_mats[h][:rank], 0.0) + jnp.where(
                cluster == home + 1, reach_mats[h][rank:], 0.0
            )

        level = [coupled(topl, group)]
        for h in range(topl - 1, -1, -1):
            wide = jnp.concatenate([m.astype(BF16) for m in level], 1)
            if h >= LOW:
                level = [mm(top_v[h, (me >> h) % 2], wide) + coupled(h, me >> h)]
                continue
            grown = mm(top_v[h].reshape(2 * rank, rank), wide)
            level = [
                grown[(c % 2) * rank:(c % 2 + 1) * rank, (c // 2) * width:(c // 2 + 1) * width]
                + coupled(h, mine_line * 2 ** (LOW - h) + c)
                for c in range(2 ** (LOW - h))
            ]
        for c, m in enumerate(level):
            gather_v[c * rank:(c + 1) * rank] = m.astype(BF16)

        for t in range(leaves):
            mat = mm_tn(trans_v[t], basis_v[t]).astype(BF16)
            spread_v[:rank, t * leaf:(t + 1) * leaf] = mat
            spread_v[rank:, t * leaf:(t + 1) * leaf] = mat
        l_near.wait()
        for t in range(leaves):
            first_v[:, t * leaf:(t + 1) * leaf] = mm(wide_x[REACH + t], near_v[t, 0])

    turn = jnp.where(rel < line // 2, 0, 1)

    def step(i, carry):
        pl.when(i == turn)(prepare)
        pl.when(i != turn)(send)
        return carry

    lax.fori_loop(0, 2, step, 0)

    def landed(buf, number, sem):
        some = buf.at[pl.ds(0, number)]
        pltpu.make_async_copy(some, some, sem).wait()

    landed(slots, line - 1, p_recv.at[0])
    held = [jnp.where(low, slots[c], slots[c + 1]) for c in range(0, line, 2)]
    parts = mm(jnp.concatenate(held, 1), gather_v[...])
    for i in range(part.shape[0]):
        part[i] = parts[:, i * 2 * rank:(i + 1) * 2 * rank]
    each_line(
        lambda e, here, l, there, i: pltpu.make_async_remote_copy(
            src_ref=part.at[here * (lines // 2) + l // 2], dst_ref=part_in.at[there * lines + own],
            send_sem=r_send.at[i], recv_sem=r_recv.at[there],
            device_id=place(e), device_id_type=MESH,
        ).start()
    )
    part_in[mine * lines + own] = part[mine * (lines // 2) + own // 2]

    l_csrc.wait()
    l_nsrc.wait()
    l_coup.wait()

    @pl.when(has_prev)
    def _():
        for copy in ups:
            copy.wait_recv()

    @pl.when(has_next)
    def _():
        for copy in downs:
            copy.wait_recv()

    anchor = me * leaves - REACH
    last = leaves + 2 * REACH

    def spot(source):
        return jnp.where(source >= 0, jnp.clip(source - anchor, 0, last - 1), last)

    sums = []
    for t in range(leaves):
        picked = [wide_c[spot(csrc_s[t, a])] for a in range(slots_adm)]
        picked = [jnp.where(low, picked[a], picked[a + 1]) for a in range(0, slots_adm, 2)]
        field = mm(
            jnp.concatenate(picked, 1), coup_v[t].reshape(slots_adm * rank, rank)
        ).astype(BF16)
        inputs = [wide_x[spot(nsrc_s[t, n])] for n in range(1, slots_near)]
        sums.append(
            mm(jnp.concatenate(inputs, 1), near_v[t, 1:].reshape(-1, leaf))
            + first_v[:, t * leaf:(t + 1) * leaf]
            + mm(field, basis_v[t])
        )

    landed(part_in, lines - 1, r_recv.at[mine])
    for _, ok, here, _ in across:
        when(ok, functools.partial(landed, part_in, lines, r_recv.at[here]))
    total = jnp.zeros((rows, 2 * rank), F32)
    for j in range(part_in.shape[0]):
        term = part_in[j]
        if groups != 2 and j // lines != 1:
            term = jnp.where(group > 0 if j < lines else group < groups - 1, term, 0.0)
        total += term
    total = jnp.where(low == (own % 2 == 0), total, 0.0)
    far = mm(total.astype(BF16), spread_v[...])
    for t in range(leaves):
        out_ref[:, t * leaf:(t + 1) * leaf] = (
            sums[t] + far[:, t * leaf:(t + 1) * leaf]
        ).astype(BF16)

    landed(slots, line - 1, p_send.at[0])
    landed(part_in, lines - 1, r_send.at[0])
    for i, (_, ok, _, _) in enumerate(across):
        when(ok, functools.partial(landed, part_in, lines, r_send.at[i + 1]))

    @pl.when(has_next)
    def _():
        for copy in ups:
            copy.wait_send()

    @pl.when(has_prev)
    def _():
        for copy in downs:
            copy.wait_send()


def solution(mesh):
    shape = tuple(mesh.shape[a] for a in AXES)
    count = shape[0] * shape[1] * shape[2]

    def local(rhs, basis, trans, coup, csrc, near, nsrc, top, cc):
        leaves, rank, leaf = basis.shape
        rows = rhs.shape[0]
        gsize = 2 ** top.shape[0]
        lines = (2 if count == 2 * gsize else 3) * gsize // 2**LOW
        args = (rhs, basis, trans, coup, csrc, near, nsrc, top, cc)

        def room(x):
            kind = pltpu.SMEM if x.dtype == jnp.int32 else pltpu.VMEM
            return kind(x.shape, x.dtype)

        dma = pltpu.SemaphoreType.DMA
        return pl.pallas_call(
            functools.partial(kernel, shape),
            out_shape=pltpu.VMEM(rhs.shape, BF16),
            in_specs=[pl.BlockSpec(memory_space=pl.ANY)] * len(args),
            out_specs=pl.BlockSpec(memory_space=pltpu.VMEM),
            scratch_shapes=[room(x) for x in args] + [
                pltpu.VMEM((leaves + 2 * REACH + 1, rows, leaf), BF16),
                pltpu.VMEM((leaves + 2 * REACH + 1, rows, 2 * rank), BF16),
                pltpu.VMEM((2**LOW, rows, 2 * rank), BF16),
                pltpu.VMEM((lines // 2, rows, 2 * rank), F32),
                pltpu.VMEM((lines, rows, 2 * rank), F32),
                pltpu.VMEM((2**LOW * rank, lines * rank), BF16),
                pltpu.VMEM((2 * rank, leaves * leaf), BF16),
                pltpu.VMEM((rows, leaves * leaf), F32),
                dma((len(args),)), dma((4,)), dma((4,)), dma((1,)), dma((1,)),
                dma((3,)), dma((3,)),
            ],
            compiler_params=pltpu.CompilerParams(collective_id=0, has_side_effects=True),
        )(*(pltpu.with_memory_space_constraint(x, pltpu.HBM) for x in args))

    placed = (
        P(None, AXES),
        P(AXES, None, None),
        P(AXES, None, None),
        P(AXES, None, None, None),
        P(AXES, None),
        P(AXES, None, None, None),
        P(AXES, None),
        P(),
        P(),
    )
    return jax.shard_map(
        local, mesh=mesh, in_specs=placed, out_specs=P(None, AXES), check_vma=False
    )
```

```python
import functools

import jax
import jax.numpy as jnp
from jax import lax
from jax.experimental import pallas as pl
from jax.experimental.pallas import tpu as pltpu
from jax.sharding import PartitionSpec as P

AXES = ("gx", "gy", "gz")
REACH = 2
LOW = 2
MESH = pl.DeviceIdType.MESH
BF16 = jnp.bfloat16
F32 = jnp.float32


def mm(a, b):
    return jnp.dot(a, b, preferred_element_type=F32)


def mm_nt(a, b):
    return lax.dot_general(a, b, (((1,), (1,)), ((), ())), preferred_element_type=F32)


def mm_tn(a, b):
    return lax.dot_general(a, b, (((0,), (0,)), ((), ())), preferred_element_type=F32)


def kernel(
    shape,
    rhs_h, basis_h, trans_h, coup_h, csrc_h, near_h, nsrc_h, top_h, cc_h,
    out_ref,
    rhs_v, basis_v, trans_v, coup_v, csrc_s, near_v, nsrc_s, top_v, cc_v,
    wide_x, wide_c, slots, part, part_in, gather_v, spread_v, first_v,
    local_sem, halo_send, halo_recv, p_send, p_recv, r_send, r_recv,
):
    nx, ny, nz = shape
    count = nx * ny * nz
    leaves, rank, leaf = basis_v.shape
    rows = rhs_v.shape[0]
    slots_near = near_v.shape[1]
    slots_adm = coup_v.shape[1]
    topl = top_v.shape[0]
    gsize = 2**topl
    groups = count // gsize
    line = 2**LOW
    lines = gsize // line
    width = part.shape[0] * 2 * rank

    me = (lax.axis_index("gx") * ny + lax.axis_index("gy")) * nz + lax.axis_index("gz")
    group = me // gsize
    mine_line = me // line
    rel = me % line
    own = mine_line % lines

    def place(e):
        return (e // (ny * nz), (e // nz) % ny, e % nz)

    loads = []
    for i, (src, dst) in enumerate(
        (
            (rhs_h, rhs_v), (basis_h, basis_v), (trans_h, trans_v), (top_h, top_v),
            (cc_h, cc_v), (csrc_h, csrc_s), (nsrc_h, nsrc_s), (coup_h, coup_v),
            (near_h, near_v),
        )
    ):
        load = pltpu.make_async_copy(src, dst, local_sem.at[i])
        load.start()
        loads.append(load)
    (l_rhs, l_basis, l_trans, l_top, l_cc, l_csrc, l_nsrc, l_coup, l_near) = loads

    if groups == 2:
        mine = group
        across = ((1 - group, None, 1 - group, group),)
    else:
        mine = 1
        across = ((group - 1, group > 0, 0, 2), (group + 1, group < groups - 1, 2, 0))
    has_prev, has_next = me > 0, me < count - 1

    def when(cond, fn):
        if cond is None:
            fn()
        else:
            pl.when(cond)(fn)

    mates = [mine_line * line + (rel ^ r) for r in range(line - 1, 0, -1)]

    def each_line(fn):
        for i, (g, ok, here, there) in enumerate(across):
            def outer(i=i, g=g, here=here, there=there):
                for k in range(lines):
                    l = own ^ k
                    fn(g * gsize + l * line + rel, here, l, there, i + 1)
            when(ok, outer)
        for k in range(lines - 1, 0, -1):
            l = own ^ k
            fn(group * gsize + l * line + rel, mine, l, mine, 0)

    barrier = pltpu.get_barrier_semaphore()

    def greet(e, *_):
        pl.semaphore_signal(barrier, inc=1, device_id=place(e), device_id_type=MESH)

    for e in mates:
        greet(e)
    out_prev = has_prev & (rel == 0)
    out_next = has_next & (rel == line - 1)
    when(out_prev, functools.partial(greet, me - 1))
    when(out_next, functools.partial(greet, me + 1))
    each_line(greet)
    expected = jnp.int32(line - 1 + lines - 1)
    expected += out_prev.astype(jnp.int32) + out_next.astype(jnp.int32)
    for _, ok, _, _ in across:
        expected += lines if ok is None else lines * ok.astype(jnp.int32)

    low = lax.broadcasted_iota(jnp.int32, (rows, 2 * rank), 1) < rank

    l_rhs.wait()
    l_basis.wait()
    coeffs = []
    for t in range(leaves):
        block = rhs_v[:, t * leaf:(t + 1) * leaf]
        basis = basis_v[t]
        both = mm_nt(block, jnp.concatenate([basis, basis], 0)).astype(BF16)
        coeffs.append(both)
    pairs = [jnp.where(low, coeffs[t], coeffs[t + 1]) for t in range(0, leaves, 2)]
    l_trans.wait()
    root = mm(jnp.concatenate(pairs, 1), trans_v[...].reshape(leaves * rank, rank)).astype(BF16)
    slots[rel] = jnp.concatenate([root, root], 1)
    for t in range(leaves):
        wide_x[REACH + t] = rhs_v[:, t * leaf:(t + 1) * leaf]
        wide_c[REACH + t] = coeffs[t]
    wide_x[leaves + 2 * REACH] = jnp.zeros((rows, leaf), BF16)
    wide_c[leaves + 2 * REACH] = jnp.zeros((rows, 2 * rank), BF16)

    def halo(buf, i, up):
        first, land = (leaves, 0) if up else (REACH, leaves + REACH)
        return pltpu.make_async_remote_copy(
            src_ref=buf.at[pl.ds(first, REACH)], dst_ref=buf.at[pl.ds(land, REACH)],
            send_sem=halo_send.at[i], recv_sem=halo_recv.at[i],
            device_id=place(me + 1 if up else me - 1), device_id_type=MESH,
        )

    ups = (halo(wide_c, 0, True), halo(wide_x, 1, True))
    downs = (halo(wide_c, 2, False), halo(wide_x, 3, False))

    def send():
        pl.semaphore_wait(barrier, expected)

        for e in mates:
            pltpu.make_async_remote_copy(
                src_ref=slots.at[rel], dst_ref=slots.at[rel],
                send_sem=p_send.at[0], recv_sem=p_recv.at[0],
                device_id=place(e), device_id_type=MESH,
            ).start()
        @pl.when(has_next)
        def _():
            for copy in ups:
                copy.start()

        @pl.when(has_prev)
        def _():
            for copy in downs:
                copy.start()

    def prepare():
        l_top.wait()
        l_cc.wait()
        lane_block = lax.broadcasted_iota(jnp.int32, (1, width), 1) // rank
        lane_group = lane_block // lines
        if groups != 2:
            lane_group = lane_group + (group - 1)
        dest = lane_group * gsize + (lane_block % lines) * line + rel
        row = lax.broadcasted_iota(jnp.int32, (rank, rank), 0)
        col = lax.broadcasted_iota(jnp.int32, (rank, rank), 1)
        down = jnp.where(row == col, 1.0, 0.0).astype(BF16)
        reach_mats = []
        for h in range(topl + 1):
            if h == 1:
                down = top_v[0, rel % 2]
            elif 1 < h <= LOW:
                down = mm(down, top_v[h - 1, (rel // 2 ** (h - 1)) % 2]).astype(BF16)
            elif h > LOW:
                down = jnp.concatenate([mm(down, top_v[h - 1, p]) for p in range(2)], 0).astype(BF16)
            stack = down if h > LOW else jnp.concatenate([down, down], 0)
            mat = mm_nt(cc_v[h].reshape(2 * rank, rank), stack)
            reach_mats.append(jnp.concatenate([mat] * (width // mat.shape[1]), 1))

        def coupled(h, cluster):
            home = dest >> h
            return jnp.where(cluster == home - 1, reach_mats[h][:rank], 0.0) + jnp.where(
                cluster == home + 1, reach_mats[h][rank:], 0.0
            )

        level = [coupled(topl, group)]
        for h in range(topl - 1, -1, -1):
            wide = jnp.concatenate([m.astype(BF16) for m in level], 1)
            if h >= LOW:
                level = [mm(top_v[h, (me >> h) % 2], wide) + coupled(h, me >> h)]
                continue
            grown = mm(top_v[h].reshape(2 * rank, rank), wide)
            level = [
                grown[(c % 2) * rank:(c % 2 + 1) * rank, (c // 2) * width:(c // 2 + 1) * width]
                + coupled(h, mine_line * 2 ** (LOW - h) + c)
                for c in range(2 ** (LOW - h))
            ]
        for c, m in enumerate(level):
            gather_v[c * rank:(c + 1) * rank] = m.astype(BF16)

        for t in range(leaves):
            mat = mm_tn(trans_v[t], basis_v[t]).astype(BF16)
            spread_v[:rank, t * leaf:(t + 1) * leaf] = mat
            spread_v[rank:, t * leaf:(t + 1) * leaf] = mat
        l_near.wait()
        for t in range(leaves):
            first_v[:, t * leaf:(t + 1) * leaf] = mm(wide_x[REACH + t], near_v[t, 0])

    turn = jnp.where(rel < line // 2, 0, 1)

    def step(i, carry):
        pl.when(i == turn)(prepare)
        pl.when(i != turn)(send)
        return carry

    lax.fori_loop(0, 2, step, 0)

    l_csrc.wait()
    l_nsrc.wait()
    l_coup.wait()

    @pl.when(has_prev)
    def _():
        for copy in ups:
            copy.wait_recv()

    @pl.when(has_next)
    def _():
        for copy in downs:
            copy.wait_recv()

    anchor = me * leaves - REACH
    last = leaves + 2 * REACH

    def spot(source):
        return jnp.where(source >= 0, jnp.clip(source - anchor, 0, last - 1), last)

    for t in range(leaves):
        picked = [wide_c[spot(csrc_s[t, a])] for a in range(slots_adm)]
        picked = [jnp.where(low, picked[a], picked[a + 1]) for a in range(0, slots_adm, 2)]
        field = mm(
            jnp.concatenate(picked, 1), coup_v[t].reshape(slots_adm * rank, rank)
        ).astype(BF16)
        inputs = [wide_x[spot(nsrc_s[t, n])] for n in range(1, slots_near)]
        first_v[:, t * leaf:(t + 1) * leaf] += (
            mm(jnp.concatenate(inputs, 1), near_v[t, 1:].reshape(-1, leaf))
            + mm(field, basis_v[t])
        )

    def landed(buf, number, sem):
        some = buf.at[pl.ds(0, number)]
        pltpu.make_async_copy(some, some, sem).wait()

    landed(slots, line - 1, p_recv.at[0])
    held = [jnp.where(low, slots[c], slots[c + 1]) for c in range(0, line, 2)]
    parts = mm(jnp.concatenate(held, 1), gather_v[...])
    for i in range(part.shape[0]):
        part[i] = parts[:, i * 2 * rank:(i + 1) * 2 * rank]
    each_line(
        lambda e, here, l, there, i: pltpu.make_async_remote_copy(
            src_ref=part.at[here * (lines // 2) + l // 2], dst_ref=part_in.at[there * lines + own],
            send_sem=r_send.at[i], recv_sem=r_recv.at[there],
            device_id=place(e), device_id_type=MESH,
        ).start()
    )
    part_in[mine * lines + own] = part[mine * (lines // 2) + own // 2]

    landed(part_in, lines - 1, r_recv.at[mine])
    for _, ok, here, _ in across:
        when(ok, functools.partial(landed, part_in, lines, r_recv.at[here]))
    total = jnp.zeros((rows, 2 * rank), F32)
    for j in range(part_in.shape[0]):
        term = part_in[j]
        if groups != 2 and j // lines != 1:
            term = jnp.where(group > 0 if j < lines else group < groups - 1, term, 0.0)
        total += term
    total = jnp.where(low == (own % 2 == 0), total, 0.0)
    far = mm(total.astype(BF16), spread_v[...])
    for t in range(leaves):
        out_ref[:, t * leaf:(t + 1) * leaf] = (
            first_v[:, t * leaf:(t + 1) * leaf] + far[:, t * leaf:(t + 1) * leaf]
        ).astype(BF16)

    landed(slots, line - 1, p_send.at[0])
    landed(part_in, lines - 1, r_send.at[0])
    for i, (_, ok, _, _) in enumerate(across):
        when(ok, functools.partial(landed, part_in, lines, r_send.at[i + 1]))

    @pl.when(has_next)
    def _():
        for copy in ups:
            copy.wait_send()

    @pl.when(has_prev)
    def _():
        for copy in downs:
            copy.wait_send()


def solution(mesh):
    shape = tuple(mesh.shape[a] for a in AXES)
    count = shape[0] * shape[1] * shape[2]

    def local(rhs, basis, trans, coup, csrc, near, nsrc, top, cc):
        leaves, rank, leaf = basis.shape
        rows = rhs.shape[0]
        gsize = 2 ** top.shape[0]
        lines = (2 if count == 2 * gsize else 3) * gsize // 2**LOW
        args = (rhs, basis, trans, coup, csrc, near, nsrc, top, cc)

        def room(x):
            kind = pltpu.SMEM if x.dtype == jnp.int32 else pltpu.VMEM
            return kind(x.shape, x.dtype)

        dma = pltpu.SemaphoreType.DMA
        return pl.pallas_call(
            functools.partial(kernel, shape),
            out_shape=pltpu.VMEM(rhs.shape, BF16),
            in_specs=[pl.BlockSpec(memory_space=pl.ANY)] * len(args),
            out_specs=pl.BlockSpec(memory_space=pltpu.VMEM),
            scratch_shapes=[room(x) for x in args] + [
                pltpu.VMEM((leaves + 2 * REACH + 1, rows, leaf), BF16),
                pltpu.VMEM((leaves + 2 * REACH + 1, rows, 2 * rank), BF16),
                pltpu.VMEM((2**LOW, rows, 2 * rank), BF16),
                pltpu.VMEM((lines // 2, rows, 2 * rank), F32),
                pltpu.VMEM((lines, rows, 2 * rank), F32),
                pltpu.VMEM((2**LOW * rank, lines * rank), BF16),
                pltpu.VMEM((2 * rank, leaves * leaf), BF16),
                pltpu.VMEM((rows, leaves * leaf), F32),
                dma((len(args),)), dma((4,)), dma((4,)), dma((1,)), dma((1,)),
                dma((3,)), dma((3,)),
            ],
            compiler_params=pltpu.CompilerParams(collective_id=0, has_side_effects=True),
        )(*(pltpu.with_memory_space_constraint(x, pltpu.HBM) for x in args))

    placed = (
        P(None, AXES),
        P(AXES, None, None),
        P(AXES, None, None),
        P(AXES, None, None, None),
        P(AXES, None),
        P(AXES, None, None, None),
        P(AXES, None),
        P(),
        P(),
    )
    return jax.shard_map(
        local, mesh=mesh, in_specs=placed, out_specs=P(None, AXES), check_vma=False
    )
```

```python
import functools

import jax
import jax.numpy as jnp
from jax import lax
from jax.experimental import pallas as pl
from jax.experimental.pallas import tpu as pltpu
from jax.sharding import PartitionSpec as P

AXES = ("gx", "gy", "gz")
REACH = 2
LOW = 2
MESH = pl.DeviceIdType.MESH
BF16 = jnp.bfloat16
F32 = jnp.float32


def mm(a, b):
    return jnp.dot(a, b, preferred_element_type=F32)


def mm_nt(a, b):
    return lax.dot_general(a, b, (((1,), (1,)), ((), ())), preferred_element_type=F32)


def mm_tn(a, b):
    return lax.dot_general(a, b, (((0,), (0,)), ((), ())), preferred_element_type=F32)


def kernel(
    shape,
    rhs_h, basis_h, trans_h, coup_h, csrc_h, near_h, nsrc_h, top_h, cc_h,
    out_ref,
    rhs_v, basis_v, trans_v, coup_v, csrc_s, near_v, nsrc_s, top_v, cc_v,
    low_x, low_c, high_x, high_c, slots,
    local_sem, halo_send, halo_recv, p_send, p_recv,
):
    nx, ny, nz = shape
    count = nx * ny * nz
    leaves, rank, leaf = basis_v.shape
    rows = rhs_v.shape[0]
    slots_near = near_v.shape[1]
    slots_adm = coup_v.shape[1]
    topl = top_v.shape[0]
    gsize = 2**topl
    groups = count // gsize
    blocks = 2 if groups == 2 else 4
    width = blocks * rank

    me = (lax.axis_index("gx") * ny + lax.axis_index("gy")) * nz + lax.axis_index("gz")
    group = me // gsize
    line = 2**LOW
    lines = gsize // line
    own = me % gsize // line
    pos = me % line

    def place(e):
        return (e // (ny * nz), (e // nz) % ny, e % nz)

    loads = []
    for i, (src, dst) in enumerate(
        (
            (rhs_h, rhs_v), (basis_h, basis_v), (trans_h, trans_v), (top_h, top_v),
            (cc_h, cc_v), (csrc_h, csrc_s), (nsrc_h, nsrc_s), (coup_h, coup_v),
            (near_h, near_v),
        )
    ):
        load = pltpu.make_async_copy(src, dst, local_sem.at[i])
        load.start()
        loads.append(load)
    (l_rhs, l_basis, l_trans, l_top, l_cc, l_csrc, l_nsrc, l_coup, l_near) = loads

    if groups == 2:
        mine = group
        across = ((1 - group, None, 1 - group, group),)
    else:
        mine = 1
        across = ((group - 1, group > 0, 0, 2), (group + 1, group < groups - 1, 2, 0))
    has_prev, has_next = me > 0, me < count - 1

    def when(cond, fn):
        if cond is None:
            fn()
        else:
            pl.when(cond)(fn)

    def each_of(q, fn):
        for i, (g, ok, _, there) in enumerate(across):
            def outer(i=i, g=g, there=there):
                for k in range(lines):
                    fn(g * gsize + (own ^ k) * line + q, there, i + 1)
            when(ok, outer)
        for k in range(lines - 1, 0, -1):
            fn(group * gsize + (own ^ k) * line + q, mine, 0)
        pl.when(pos != q)(lambda: fn(group * gsize + own * line + q, mine, 0))

    barrier = pltpu.get_barrier_semaphore()

    def greet(e, *_):
        pl.semaphore_signal(barrier, inc=1, device_id=place(e), device_id_type=MESH)

    for q in range(line - 1, -1, -1):
        pl.when(q >= pos)(functools.partial(each_of, q, greet))
    expected = jnp.int32(lines)
    for _, ok, _, _ in across:
        expected += lines if ok is None else lines * ok.astype(jnp.int32)
    expected = expected * (pos + 1) - 1

    low = lax.broadcasted_iota(jnp.int32, (rows, 2 * rank), 1) < rank

    l_rhs.wait()
    l_basis.wait()
    coeffs = []
    for t in range(leaves):
        block = rhs_v[:, t * leaf:(t + 1) * leaf]
        basis = basis_v[t]
        both = mm_nt(block, jnp.concatenate([basis, basis], 0)).astype(BF16)
        coeffs.append(both)
    pairs = [jnp.where(low, coeffs[t], coeffs[t + 1]) for t in range(0, leaves, 2)]
    l_trans.wait()
    root = mm(jnp.concatenate(pairs, 1), trans_v[...].reshape(leaves * rank, rank)).astype(BF16)
    slots[mine, pos, own] = jnp.concatenate([root, root], 1)

    pl.semaphore_wait(barrier, expected)

    def send(q):
        each_of(
            q,
            lambda e, there, i: pltpu.make_async_remote_copy(
                src_ref=slots.at[mine, pos, own], dst_ref=slots.at[there, pos, own],
                send_sem=p_send.at[i, q], recv_sem=p_recv.at[there, pos],
                device_id=place(e), device_id_type=MESH,
            ).start(),
        )

    def landed(block, q, number, sem):
        some = slots.at[block, q, pl.ds(0, number)]
        pltpu.make_async_copy(some, some, sem).wait()

    def arrived(q):
        pl.when(q == pos)(functools.partial(landed, mine, q, lines - 1, p_recv.at[mine, q]))
        pl.when(q != pos)(functools.partial(landed, mine, q, lines, p_recv.at[mine, q]))
        for _, ok, here, _ in across:
            when(ok, functools.partial(landed, here, q, lines, p_recv.at[here, q]))

    def halo(src, first, dst, land, i, up):
        return pltpu.make_async_remote_copy(
            src_ref=src.at[pl.ds(first, REACH)], dst_ref=dst.at[pl.ds(land, REACH)],
            send_sem=halo_send.at[i], recv_sem=halo_recv.at[i],
            device_id=place(me + 1 if up else me - 1), device_id_type=MESH,
        )

    ups = (halo(high_c, leaves - REACH, low_c, 0, 0, True),
           halo(high_x, leaves - REACH, low_x, 0, 1, True))
    downs = (halo(low_c, REACH, high_c, leaves, 2, False),
             halo(low_x, REACH, high_x, leaves, 3, False))

    def start(copies):
        for copy in copies:
            copy.start()

    for q in range(line):
        pl.when(q <= pos)(functools.partial(send, q))
    for t in range(leaves):
        for ref, at in ((low_x, REACH + t), (high_x, t)):
            ref[at] = rhs_v[:, t * leaf:(t + 1) * leaf]
        for ref, at in ((low_c, REACH + t), (high_c, t)):
            ref[at] = coeffs[t]
    for ref in (low_x, high_x, low_c, high_c):
        ref[leaves + REACH] = jnp.zeros(ref.shape[1:], BF16)
    pl.when(has_next & (pos == line - 1))(functools.partial(start, ups))
    pl.when(has_prev & (pos > 0))(functools.partial(start, downs))

    l_top.wait()
    l_cc.wait()
    lane_block = lax.broadcasted_iota(jnp.int32, (1, width), 1) // rank
    if groups == 2:
        lane_group = lane_block
    else:
        lane_group = jnp.where(lane_block < 3, group - 1 + lane_block, -8)
    row = lax.broadcasted_iota(jnp.int32, (rank, rank), 0)
    col = lax.broadcasted_iota(jnp.int32, (rank, rank), 1)
    down = jnp.where(row == col, 1.0, 0.0).astype(BF16)
    reach_mats = []
    for h in range(topl + 1):
        if h == 1:
            down = top_v[0, me % 2]
        elif h > 1:
            down = mm(down, top_v[h - 1, (me // 2 ** (h - 1)) % 2]).astype(BF16)
        reach_mats.append(
            mm_nt(cc_v[h].reshape(2 * rank, rank), jnp.concatenate([down] * blocks, 0))
        )

    def coupled(h, c):
        cluster = lane_group * 2 ** (topl - h) + c
        home = me // 2**h
        return jnp.where(cluster == home - 1, reach_mats[h][:rank], 0.0) + jnp.where(
            cluster == home + 1, reach_mats[h][rank:], 0.0
        )

    level = [coupled(topl, 0)]
    for h in range(topl - 1, -1, -1):
        wide = jnp.concatenate([m.astype(BF16) for m in level], 1)
        grown = mm(top_v[h].reshape(2 * rank, rank), wide)
        level = [
            grown[(c % 2) * rank:(c % 2 + 1) * rank, (c // 2) * width:(c // 2 + 1) * width]
            + coupled(h, c)
            for c in range(2 ** (topl - h))
        ]
    gather_mat = jnp.concatenate([m.astype(BF16) for m in level], 0)

    spread = [mm_tn(trans_v[t], basis_v[t]).astype(BF16) for t in range(leaves)]
    spread = jnp.concatenate(spread, 1)
    spread = jnp.concatenate([spread] * blocks, 0)

    l_csrc.wait()
    l_nsrc.wait()
    l_coup.wait()
    l_near.wait()
    sums = [
        mm(rhs_v[:, t * leaf:(t + 1) * leaf], near_v[t, 0]) for t in range(leaves)
    ]

    def meet(q):
        arrived(q)
        send(q)
        if q == line - 1:
            pl.when(has_prev & (pos == 0))(functools.partial(start, downs))
        pl.when(has_next & (pos == q - 1))(functools.partial(start, ups))

    def neighbours(t, wide_x, wide_c, anchor):
        def spot(source):
            inside = jnp.clip(source - anchor, 0, leaves + REACH - 1)
            return jnp.where(source >= 0, inside, leaves + REACH)

        picked = [wide_c[spot(csrc_s[t, a])] for a in range(slots_adm)]
        picked = [jnp.where(low, picked[a], picked[a + 1]) for a in range(0, slots_adm, 2)]
        field = mm(
            jnp.concatenate(picked, 1), coup_v[t].reshape(slots_adm * rank, rank)
        ).astype(BF16)
        inputs = [wide_x[spot(nsrc_s[t, n])] for n in range(1, slots_near)]
        return mm(jnp.concatenate(inputs, 1), near_v[t, 1:].reshape(-1, leaf)) + mm(
            field, basis_v[t]
        )

    def receive(copies):
        for copy in copies:
            copy.wait_recv()

    for q in range(1, line - 1):
        pl.when(q > pos)(functools.partial(meet, q))

    pl.when(has_next)(functools.partial(receive, downs))
    for t in range(REACH, leaves):
        sums[t] += neighbours(t, high_x, high_c, me * leaves)

    pl.when(line - 1 > pos)(functools.partial(meet, line - 1))

    pl.when(has_prev)(functools.partial(receive, ups))
    for t in range(REACH):
        sums[t] += neighbours(t, low_x, low_c, me * leaves - REACH)

    for q in range(line):
        pl.when(q <= pos)(functools.partial(arrived, q))
    used = 2 if groups == 2 else 3
    held = [
        jnp.concatenate(
            [
                jnp.where(low, slots[b, c % line, c // line], slots[b, c % line + 1, c // line])
                for c in range(0, gsize, 2)
            ],
            1,
        )
        for b in range(used)
    ]
    fields = mm(jnp.concatenate(held, 0), gather_mat)
    cells = lax.broadcasted_iota(jnp.int32, (rows, width), 1) // rank
    total = jnp.zeros((rows, width), F32)
    for b in range(used):
        ours = cells == b
        if groups != 2 and b != 1:
            ours = ours & (group > 0 if b == 0 else group < groups - 1)
        total = jnp.where(ours, fields[b * rows:(b + 1) * rows], total)
    far = mm(total.astype(BF16), spread)
    for t in range(leaves):
        out_ref[:, t * leaf:(t + 1) * leaf] = (
            sums[t] + far[:, t * leaf:(t + 1) * leaf]
        ).astype(BF16)

    for q in range(line):
        pl.when(q == pos)(functools.partial(landed, mine, q, lines - 1, p_send.at[0, q]))
        pl.when(q != pos)(functools.partial(landed, mine, q, lines, p_send.at[0, q]))
        for i, (_, ok, here, _) in enumerate(across):
            when(ok, functools.partial(landed, here, q, lines, p_send.at[i + 1, q]))

    @pl.when(has_next)
    def _():
        for copy in ups:
            copy.wait_send()

    @pl.when(has_prev)
    def _():
        for copy in downs:
            copy.wait_send()


def solution(mesh):
    shape = tuple(mesh.shape[a] for a in AXES)
    count = shape[0] * shape[1] * shape[2]

    def local(rhs, basis, trans, coup, csrc, near, nsrc, top, cc):
        leaves, rank, leaf = basis.shape
        rows = rhs.shape[0]
        gsize = 2 ** top.shape[0]
        blocks = 2 if count == 2 * gsize else 4
        args = (rhs, basis, trans, coup, csrc, near, nsrc, top, cc)

        def room(x):
            kind = pltpu.SMEM if x.dtype == jnp.int32 else pltpu.VMEM
            return kind(x.shape, x.dtype)

        dma = pltpu.SemaphoreType.DMA
        return pl.pallas_call(
            functools.partial(kernel, shape),
            out_shape=pltpu.VMEM(rhs.shape, BF16),
            in_specs=[pl.BlockSpec(memory_space=pl.ANY)] * len(args),
            out_specs=pl.BlockSpec(memory_space=pltpu.VMEM),
            scratch_shapes=[room(x) for x in args] + [
                pltpu.VMEM((leaves + REACH + 1, rows, leaf), BF16),
                pltpu.VMEM((leaves + REACH + 1, rows, 2 * rank), BF16),
                pltpu.VMEM((leaves + REACH + 1, rows, leaf), BF16),
                pltpu.VMEM((leaves + REACH + 1, rows, 2 * rank), BF16),
                pltpu.VMEM((blocks, 2**LOW, gsize // 2**LOW, rows, 2 * rank), BF16),
                dma((len(args),)), dma((4,)), dma((4,)), dma((3, 2**LOW)), dma((blocks, 2**LOW)),
            ],
            compiler_params=pltpu.CompilerParams(collective_id=0, has_side_effects=True),
        )(*(pltpu.with_memory_space_constraint(x, pltpu.HBM) for x in args))

    placed = (
        P(None, AXES),
        P(AXES, None, None),
        P(AXES, None, None),
        P(AXES, None, None, None),
        P(AXES, None),
        P(AXES, None, None, None),
        P(AXES, None),
        P(),
        P(),
    )
    return jax.shard_map(
        local, mesh=mesh, in_specs=placed, out_specs=P(None, AXES), check_vma=False
    )
```

```python
import functools

import jax
import jax.numpy as jnp
from jax import lax
from jax.experimental import pallas as pl
from jax.experimental.pallas import tpu as pltpu
from jax.sharding import PartitionSpec as P

AXES = ("gx", "gy", "gz")
REACH = 2
LOW = 2
MESH = pl.DeviceIdType.MESH
BF16 = jnp.bfloat16
F32 = jnp.float32


def mm(a, b):
    return jnp.dot(a, b, preferred_element_type=F32)


def mm_nt(a, b):
    return lax.dot_general(a, b, (((1,), (1,)), ((), ())), preferred_element_type=F32)


def mm_tn(a, b):
    return lax.dot_general(a, b, (((0,), (0,)), ((), ())), preferred_element_type=F32)


def kernel(
    shape,
    rhs_h, basis_h, trans_h, coup_h, csrc_h, near_h, nsrc_h, top_h, cc_h,
    out_ref,
    rhs_v, basis_v, trans_v, coup_v, csrc_s, near_v, nsrc_s, top_v, cc_v,
    wide_x, wide_c, slots, part, part_in, gather_v, spread_v, first_v,
    local_sem, halo_send, halo_recv, p_send, p_recv, r_send, r_recv,
):
    nx, ny, nz = shape
    count = nx * ny * nz
    leaves, rank, leaf = basis_v.shape
    rows = rhs_v.shape[0]
    slots_near = near_v.shape[1]
    slots_adm = coup_v.shape[1]
    topl = top_v.shape[0]
    gsize = 2**topl
    groups = count // gsize
    line = 2**LOW
    lines = gsize // line
    width = part.shape[0] * 2 * rank

    me = (lax.axis_index("gx") * ny + lax.axis_index("gy")) * nz + lax.axis_index("gz")
    group = me // gsize
    mine_line = me // line
    rel = me % line
    own = mine_line % lines

    def place(e):
        return (e // (ny * nz), (e // nz) % ny, e % nz)

    loads = []
    for i, (src, dst) in enumerate(
        (
            (rhs_h, rhs_v), (basis_h, basis_v), (trans_h, trans_v), (top_h, top_v),
            (cc_h, cc_v), (csrc_h, csrc_s), (nsrc_h, nsrc_s), (coup_h, coup_v),
            (near_h, near_v),
        )
    ):
        load = pltpu.make_async_copy(src, dst, local_sem.at[i])
        if i < 3:
            load.start()
        loads.append(load)
    (l_rhs, l_basis, l_trans, l_top, l_cc, l_csrc, l_nsrc, l_coup, l_near) = loads

    if groups == 2:
        mine = group
        across = ((1 - group, None, 1 - group, group),)
    else:
        mine = 1
        across = ((group - 1, group > 0, 0, 2), (group + 1, group < groups - 1, 2, 0))
    has_prev, has_next = me > 0, me < count - 1

    def when(cond, fn):
        if cond is None:
            fn()
        else:
            pl.when(cond)(fn)

    def to_mate(q):
        return pltpu.make_async_remote_copy(
            src_ref=slots.at[rel], dst_ref=slots.at[rel],
            send_sem=p_send.at[q], recv_sem=p_recv.at[rel],
            device_id=place(mine_line * line + q), device_id_type=MESH,
        )

    def from_mate(q):
        return pltpu.make_async_copy(slots.at[q], slots.at[q], p_recv.at[q])

    def each_line(fn):
        for i, (g, ok, here, there) in enumerate(across):
            def outer(i=i, g=g, here=here, there=there):
                for k in range(lines):
                    l = own ^ k
                    fn(g * gsize + l * line + rel, here, l, there, i + 1)
            when(ok, outer)
        for k in range(lines - 1, 0, -1):
            l = own ^ k
            fn(group * gsize + l * line + rel, mine, l, mine, 0)

    barrier = pltpu.get_barrier_semaphore()

    def greet(e, *_):
        pl.semaphore_signal(barrier, inc=1, device_id=place(e), device_id_type=MESH)

    for r in range(line - 1, 0, -1):
        pl.when((rel ^ r) > rel)(functools.partial(greet, mine_line * line + (rel ^ r)))
    out_prev = has_prev & (rel == 0)
    out_next = has_next & (rel == line - 1)
    when(out_prev, functools.partial(greet, me - 1))
    each_line(greet)
    expected = rel + lines - 1 + out_next.astype(jnp.int32)
    for _, ok, _, _ in across:
        expected += lines if ok is None else lines * ok.astype(jnp.int32)

    wide_x[leaves + 2 * REACH] = jnp.zeros((rows, leaf), BF16)
    wide_c[leaves + 2 * REACH] = jnp.zeros((rows, 2 * rank), BF16)
    low = lax.broadcasted_iota(jnp.int32, (rows, 2 * rank), 1) < rank

    l_rhs.wait()
    l_basis.wait()
    coeffs = []
    for t in range(leaves):
        block = rhs_v[:, t * leaf:(t + 1) * leaf]
        wide_x[REACH + t] = block
        basis = basis_v[t]
        both = mm_nt(block, jnp.concatenate([basis, basis], 0)).astype(BF16)
        wide_c[REACH + t] = both
        coeffs.append(both)
    pairs = [jnp.where(low, coeffs[t], coeffs[t + 1]) for t in range(0, leaves, 2)]
    l_trans.wait()
    root = mm(jnp.concatenate(pairs, 1), trans_v[...].reshape(leaves * rank, rank)).astype(BF16)
    slots[rel] = jnp.concatenate([root, root], 1)

    def halo(buf, i, up):
        first, land = (leaves, 0) if up else (REACH, leaves + REACH)
        return pltpu.make_async_remote_copy(
            src_ref=buf.at[pl.ds(first, REACH)], dst_ref=buf.at[pl.ds(land, REACH)],
            send_sem=halo_send.at[i], recv_sem=halo_recv.at[i],
            device_id=place(me + 1 if up else me - 1), device_id_type=MESH,
        )

    ups = (halo(wide_c, 0, True), halo(wide_x, 1, True))
    downs = (halo(wide_c, 2, False), halo(wide_x, 3, False))

    def send():
        pl.semaphore_wait(barrier, expected)

        for q in range(line):
            pl.when(q < rel)(lambda q=q: to_mate(q).start())

        @pl.when(out_next)
        def _():
            for copy in ups:
                copy.start()

        @pl.when(rel > 0)
        def _():
            for copy in downs:
                copy.start()

    def prepare():
        for load in loads[3:]:
            load.start()
        l_top.wait()
        l_cc.wait()
        lane_block = lax.broadcasted_iota(jnp.int32, (1, width), 1) // rank
        lane_group = lane_block // lines
        if groups != 2:
            lane_group = lane_group + (group - 1)
        dest = lane_group * gsize + (lane_block % lines) * line + rel
        row = lax.broadcasted_iota(jnp.int32, (rank, rank), 0)
        col = lax.broadcasted_iota(jnp.int32, (rank, rank), 1)
        down = jnp.where(row == col, 1.0, 0.0).astype(BF16)
        reach_mats = []
        for h in range(topl + 1):
            if h == 1:
                down = top_v[0, rel % 2]
            elif 1 < h <= LOW:
                down = mm(down, top_v[h - 1, (rel // 2 ** (h - 1)) % 2]).astype(BF16)
            elif h > LOW:
                down = jnp.concatenate([mm(down, top_v[h - 1, p]) for p in range(2)], 0).astype(BF16)
            stack = down if h > LOW else jnp.concatenate([down, down], 0)
            mat = mm_nt(cc_v[h].reshape(2 * rank, rank), stack)
            reach_mats.append(jnp.concatenate([mat] * (width // mat.shape[1]), 1))

        def coupled(h, cluster):
            home = dest >> h
            return jnp.where(cluster == home - 1, reach_mats[h][:rank], 0.0) + jnp.where(
                cluster == home + 1, reach_mats[h][rank:], 0.0
            )

        level = [coupled(topl, group)]
        for h in range(topl - 1, -1, -1):
            wide = jnp.concatenate([m.astype(BF16) for m in level], 1)
            if h >= LOW:
                level = [mm(top_v[h, (me >> h) % 2], wide) + coupled(h, me >> h)]
                continue
            grown = mm(top_v[h].reshape(2 * rank, rank), wide)
            level = [
                grown[(c % 2) * rank:(c % 2 + 1) * rank, (c // 2) * width:(c // 2 + 1) * width]
                + coupled(h, mine_line * 2 ** (LOW - h) + c)
                for c in range(2 ** (LOW - h))
            ]
        for c, m in enumerate(level):
            gather_v[c * rank:(c + 1) * rank] = m.astype(BF16)

        for t in range(leaves):
            mat = mm_tn(trans_v[t], basis_v[t]).astype(BF16)
            spread_v[:rank, t * leaf:(t + 1) * leaf] = mat
            spread_v[rank:, t * leaf:(t + 1) * leaf] = mat
        l_near.wait()
        for t in range(leaves):
            first_v[:, t * leaf:(t + 1) * leaf] = mm(wide_x[REACH + t], near_v[t, 0])

    turn = jnp.where(rel < line // 2, 0, 1)

    def step(i, carry):
        pl.when(i == turn)(prepare)
        pl.when(i != turn)(send)
        return carry

    lax.fori_loop(0, 2, step, 0)

    def landed(buf, number, sem):
        some = buf.at[pl.ds(0, number)]
        pltpu.make_async_copy(some, some, sem).wait()

    for q in range(1, line):
        @pl.when(q > rel)
        def _(q=q):
            from_mate(q).wait()
            to_mate(q).start()

        @pl.when(q - 1 == rel)
        def _():
            for copy in ups:
                copy.start()

    for q in range(line):
        pl.when(q < rel)(lambda q=q: from_mate(q).wait())
    held = [jnp.where(low, slots[c], slots[c + 1]) for c in range(0, line, 2)]
    parts = mm(jnp.concatenate(held, 1), gather_v[...])
    for i in range(part.shape[0]):
        part[i] = parts[:, i * 2 * rank:(i + 1) * 2 * rank].astype(BF16)
    each_line(
        lambda e, here, l, there, i: pltpu.make_async_remote_copy(
            src_ref=part.at[here * (lines // 2) + l // 2], dst_ref=part_in.at[there * lines + own],
            send_sem=r_send.at[i], recv_sem=r_recv.at[there],
            device_id=place(e), device_id_type=MESH,
        ).start()
    )
    part_in[mine * lines + own] = part[mine * (lines // 2) + own // 2]

    l_csrc.wait()
    l_nsrc.wait()
    l_coup.wait()

    @pl.when(has_prev)
    def _():
        for copy in ups:
            copy.wait_recv()

    @pl.when(out_prev)
    def _():
        for copy in downs:
            copy.start()

    @pl.when(has_next)
    def _():
        for copy in downs:
            copy.wait_recv()

    anchor = me * leaves - REACH
    last = leaves + 2 * REACH

    def spot(source):
        return jnp.where(source >= 0, jnp.clip(source - anchor, 0, last - 1), last)

    sums = []
    for t in range(leaves):
        picked = [wide_c[spot(csrc_s[t, a])] for a in range(slots_adm)]
        picked = [jnp.where(low, picked[a], picked[a + 1]) for a in range(0, slots_adm, 2)]
        field = mm(
            jnp.concatenate(picked, 1), coup_v[t].reshape(slots_adm * rank, rank)
        ).astype(BF16)
        inputs = [wide_x[spot(nsrc_s[t, n])] for n in range(1, slots_near)]
        sums.append(
            mm(jnp.concatenate(inputs, 1), near_v[t, 1:].reshape(-1, leaf))
            + first_v[:, t * leaf:(t + 1) * leaf]
            + mm(field, basis_v[t])
        )

    landed(part_in, lines - 1, r_recv.at[mine])
    for _, ok, here, _ in across:
        when(ok, functools.partial(landed, part_in, lines, r_recv.at[here]))
    total = jnp.zeros((rows, 2 * rank), F32)
    for j in range(part_in.shape[0]):
        term = part_in[j].astype(F32)
        if groups != 2 and j // lines != 1:
            term = jnp.where(group > 0 if j < lines else group < groups - 1, term, 0.0)
        total += term
    total = jnp.where(low == (own % 2 == 0), total, 0.0)
    far = mm(total.astype(BF16), spread_v[...])
    for t in range(leaves):
        out_ref[:, t * leaf:(t + 1) * leaf] = (
            sums[t] + far[:, t * leaf:(t + 1) * leaf]
        ).astype(BF16)

    for q in range(line):
        pl.when(q != rel)(lambda q=q: to_mate(q).wait_send())
    landed(part_in, lines - 1, r_send.at[0])
    for i, (_, ok, _, _) in enumerate(across):
        when(ok, functools.partial(landed, part_in, lines, r_send.at[i + 1]))

    @pl.when(has_next)
    def _():
        for copy in ups:
            copy.wait_send()

    @pl.when(has_prev)
    def _():
        for copy in downs:
            copy.wait_send()


def solution(mesh):
    shape = tuple(mesh.shape[a] for a in AXES)
    count = shape[0] * shape[1] * shape[2]

    def local(rhs, basis, trans, coup, csrc, near, nsrc, top, cc):
        leaves, rank, leaf = basis.shape
        rows = rhs.shape[0]
        gsize = 2 ** top.shape[0]
        lines = (2 if count == 2 * gsize else 3) * gsize // 2**LOW
        args = (rhs, basis, trans, coup, csrc, near, nsrc, top, cc)

        def room(x):
            kind = pltpu.SMEM if x.dtype == jnp.int32 else pltpu.VMEM
            return kind(x.shape, x.dtype)

        dma = pltpu.SemaphoreType.DMA
        return pl.pallas_call(
            functools.partial(kernel, shape),
            out_shape=pltpu.VMEM(rhs.shape, BF16),
            in_specs=[pl.BlockSpec(memory_space=pl.ANY)] * len(args),
            out_specs=pl.BlockSpec(memory_space=pltpu.VMEM),
            scratch_shapes=[room(x) for x in args] + [
                pltpu.VMEM((leaves + 2 * REACH + 1, rows, leaf), BF16),
                pltpu.VMEM((leaves + 2 * REACH + 1, rows, 2 * rank), BF16),
                pltpu.VMEM((2**LOW, rows, 2 * rank), BF16),
                pltpu.VMEM((lines // 2, rows, 2 * rank), BF16),
                pltpu.VMEM((lines, rows, 2 * rank), BF16),
                pltpu.VMEM((2**LOW * rank, lines * rank), BF16),
                pltpu.VMEM((2 * rank, leaves * leaf), BF16),
                pltpu.VMEM((rows, leaves * leaf), F32),
                dma((len(args),)), dma((4,)), dma((4,)), dma((2**LOW,)), dma((2**LOW,)),
                dma((3,)), dma((3,)),
            ],
            compiler_params=pltpu.CompilerParams(collective_id=0, has_side_effects=True),
        )(*(pltpu.with_memory_space_constraint(x, pltpu.HBM) for x in args))

    placed = (
        P(None, AXES),
        P(AXES, None, None),
        P(AXES, None, None),
        P(AXES, None, None, None),
        P(AXES, None),
        P(AXES, None, None, None),
        P(AXES, None),
        P(),
        P(),
    )
    return jax.shard_map(
        local, mesh=mesh, in_specs=placed, out_specs=P(None, AXES), check_vma=False
    )
```

```python
import functools

import jax
import jax.numpy as jnp
from jax import lax
from jax.experimental import pallas as pl
from jax.experimental.pallas import tpu as pltpu
from jax.sharding import PartitionSpec as P

AXES = ("gx", "gy", "gz")
REACH = 2
LOW = 2
MESH = pl.DeviceIdType.MESH
BF16 = jnp.bfloat16
F32 = jnp.float32


def mm(a, b):
    return jnp.dot(a, b, preferred_element_type=F32)


def mm_nt(a, b):
    return lax.dot_general(a, b, (((1,), (1,)), ((), ())), preferred_element_type=F32)


def mm_tn(a, b):
    return lax.dot_general(a, b, (((0,), (0,)), ((), ())), preferred_element_type=F32)


def kernel(
    shape,
    rhs_h, basis_h, trans_h, coup_h, csrc_h, near_h, nsrc_h, top_h, cc_h,
    out_ref,
    rhs_v, basis_v, trans_v, coup_v, csrc_s, near_v, nsrc_s, top_v, cc_v,
    wide_x, wide_c, slots, part, part_in, gather_v, spread_v, first_v,
    local_sem, halo_send, halo_recv, p_send, p_recv, r_send, r_recv,
):
    nx, ny, nz = shape
    count = nx * ny * nz
    leaves, rank, leaf = basis_v.shape
    rows = rhs_v.shape[0]
    slots_near = near_v.shape[1]
    slots_adm = coup_v.shape[1]
    topl = top_v.shape[0]
    gsize = 2**topl
    groups = count // gsize
    line = 2**LOW
    lines = gsize // line
    width = part.shape[0] * 2 * rank

    me = (lax.axis_index("gx") * ny + lax.axis_index("gy")) * nz + lax.axis_index("gz")
    group = me // gsize
    mine_line = me // line
    rel = me % line
    own = mine_line % lines

    def place(e):
        return (e // (ny * nz), (e // nz) % ny, e % nz)

    loads = []
    for i, (src, dst) in enumerate(
        (
            (rhs_h, rhs_v), (basis_h, basis_v), (trans_h, trans_v), (top_h, top_v),
            (cc_h, cc_v), (csrc_h, csrc_s), (nsrc_h, nsrc_s), (coup_h, coup_v),
            (near_h, near_v),
        )
    ):
        load = pltpu.make_async_copy(src, dst, local_sem.at[i])
        if i < 3:
            load.start()
        loads.append(load)
    (l_rhs, l_basis, l_trans, l_top, l_cc, l_csrc, l_nsrc, l_coup, l_near) = loads

    if groups == 2:
        mine = group
        across = ((1 - group, None, 1 - group, group),)
    else:
        mine = 1
        across = ((group - 1, group > 0, 0, 2), (group + 1, group < groups - 1, 2, 0))
    has_prev, has_next = me > 0, me < count - 1

    def when(cond, fn):
        if cond is None:
            fn()
        else:
            pl.when(cond)(fn)

    def to_mate(q):
        return pltpu.make_async_remote_copy(
            src_ref=slots.at[rel], dst_ref=slots.at[rel],
            send_sem=p_send.at[q], recv_sem=p_recv.at[rel],
            device_id=place(mine_line * line + q), device_id_type=MESH,
        )

    def from_mate(q):
        return pltpu.make_async_copy(slots.at[q], slots.at[q], p_recv.at[q])

    def each_line(fn):
        for i, (g, ok, here, there) in enumerate(across):
            def outer(i=i, g=g, here=here, there=there):
                for k in range(lines):
                    l = own ^ k
                    fn(g * gsize + l * line + rel, here, l, there, i + 1)
            when(ok, outer)
        for k in range(lines - 1, 0, -1):
            l = own ^ k
            fn(group * gsize + l * line + rel, mine, l, mine, 0)

    barrier = pltpu.get_barrier_semaphore()

    def greet(e, *_):
        pl.semaphore_signal(barrier, inc=1, device_id=place(e), device_id_type=MESH)

    for r in range(line - 1, 0, -1):
        pl.when((rel ^ r) > rel)(functools.partial(greet, mine_line * line + (rel ^ r)))
    out_prev = has_prev & (rel == 0)
    out_next = has_next & (rel == line - 1)
    when(out_prev, functools.partial(greet, me - 1))
    each_line(greet)
    expected = rel + lines - 1 + out_next.astype(jnp.int32)
    for _, ok, _, _ in across:
        expected += lines if ok is None else lines * ok.astype(jnp.int32)

    wide_x[leaves + 2 * REACH] = jnp.zeros((rows, leaf), BF16)
    wide_c[leaves + 2 * REACH] = jnp.zeros((rows, 2 * rank), BF16)
    low = lax.broadcasted_iota(jnp.int32, (rows, 2 * rank), 1) < rank

    l_rhs.wait()
    l_basis.wait()
    coeffs = []
    for t in range(leaves):
        block = rhs_v[:, t * leaf:(t + 1) * leaf]
        wide_x[REACH + t] = block
        basis = basis_v[t]
        both = mm_nt(block, jnp.concatenate([basis, basis], 0)).astype(BF16)
        wide_c[REACH + t] = both
        coeffs.append(both)
    pairs = [jnp.where(low, coeffs[t], coeffs[t + 1]) for t in range(0, leaves, 2)]
    l_trans.wait()
    root = mm(jnp.concatenate(pairs, 1), trans_v[...].reshape(leaves * rank, rank)).astype(BF16)
    slots[rel] = jnp.concatenate([root, root], 1)

    def halo(buf, i, up):
        first, land = (leaves, 0) if up else (REACH, leaves + REACH)
        return pltpu.make_async_remote_copy(
            src_ref=buf.at[pl.ds(first, REACH)], dst_ref=buf.at[pl.ds(land, REACH)],
            send_sem=halo_send.at[i], recv_sem=halo_recv.at[i],
            device_id=place(me + 1 if up else me - 1), device_id_type=MESH,
        )

    ups = (halo(wide_c, 0, True), halo(wide_x, 1, True))
    downs = (halo(wide_c, 2, False), halo(wide_x, 3, False))

    def send():
        pl.semaphore_wait(barrier, expected)

        for q in range(line):
            pl.when(q < rel)(lambda q=q: to_mate(q).start())

        @pl.when(out_next)
        def _():
            for copy in ups:
                copy.start()

        @pl.when(rel > 0)
        def _():
            for copy in downs:
                copy.start()

    def prepare():
        for load in loads[3:]:
            load.start()
        l_top.wait()
        l_cc.wait()
        lane_block = lax.broadcasted_iota(jnp.int32, (1, width), 1) // rank
        lane_group = lane_block // lines
        if groups != 2:
            lane_group = lane_group + (group - 1)
        dest = lane_group * gsize + (lane_block % lines) * line + rel
        row = lax.broadcasted_iota(jnp.int32, (rank, rank), 0)
        col = lax.broadcasted_iota(jnp.int32, (rank, rank), 1)
        down = jnp.where(row == col, 1.0, 0.0).astype(BF16)
        reach_mats = []
        for h in range(topl + 1):
            if h == 1:
                down = top_v[0, rel % 2]
            elif 1 < h <= LOW:
                down = mm(down, top_v[h - 1, (rel // 2 ** (h - 1)) % 2]).astype(BF16)
            elif h > LOW:
                down = jnp.concatenate([mm(down, top_v[h - 1, p]) for p in range(2)], 0).astype(BF16)
            stack = down if h > LOW else jnp.concatenate([down, down], 0)
            mat = mm_nt(cc_v[h].reshape(2 * rank, rank), stack)
            reach_mats.append(jnp.concatenate([mat] * (width // mat.shape[1]), 1))

        def coupled(h, cluster):
            home = dest >> h
            return jnp.where(cluster == home - 1, reach_mats[h][:rank], 0.0) + jnp.where(
                cluster == home + 1, reach_mats[h][rank:], 0.0
            )

        level = [coupled(topl, group)]
        for h in range(topl - 1, -1, -1):
            wide = jnp.concatenate([m.astype(BF16) for m in level], 1)
            if h >= LOW:
                level = [mm(top_v[h, (me >> h) % 2], wide) + coupled(h, me >> h)]
                continue
            grown = mm(top_v[h].reshape(2 * rank, rank), wide)
            level = [
                grown[(c % 2) * rank:(c % 2 + 1) * rank, (c // 2) * width:(c // 2 + 1) * width]
                + coupled(h, mine_line * 2 ** (LOW - h) + c)
                for c in range(2 ** (LOW - h))
            ]
        for c, m in enumerate(level):
            gather_v[c * rank:(c + 1) * rank] = m.astype(BF16)

        for t in range(leaves):
            mat = mm_tn(trans_v[t], basis_v[t]).astype(BF16)
            spread_v[:rank, t * leaf:(t + 1) * leaf] = mat
            spread_v[rank:, t * leaf:(t + 1) * leaf] = mat
        l_near.wait()
        for t in range(leaves):
            first_v[:, t * leaf:(t + 1) * leaf] = mm(wide_x[REACH + t], near_v[t, 0])

    turn = jnp.where(rel == 0, 0, 1)

    def step(i, carry):
        pl.when(i == turn)(prepare)
        pl.when(i != turn)(send)
        return carry

    lax.fori_loop(0, 2, step, 0)

    def landed(buf, number, sem):
        some = buf.at[pl.ds(0, number)]
        pltpu.make_async_copy(some, some, sem).wait()

    for q in range(1, line):
        @pl.when(q > rel)
        def _(q=q):
            from_mate(q).wait()
            to_mate(q).start()

        @pl.when(q - 1 == rel)
        def _():
            for copy in ups:
                copy.start()

    for q in range(line):
        pl.when(q < rel)(lambda q=q: from_mate(q).wait())
    held = [jnp.where(low, slots[c], slots[c + 1]) for c in range(0, line, 2)]
    parts = mm(jnp.concatenate(held, 1), gather_v[...])
    for i in range(part.shape[0]):
        part[i] = parts[:, i * 2 * rank:(i + 1) * 2 * rank].astype(BF16)
    each_line(
        lambda e, here, l, there, i: pltpu.make_async_remote_copy(
            src_ref=part.at[here * (lines // 2) + l // 2], dst_ref=part_in.at[there * lines + own],
            send_sem=r_send.at[i], recv_sem=r_recv.at[there],
            device_id=place(e), device_id_type=MESH,
        ).start()
    )
    part_in[mine * lines + own] = part[mine * (lines // 2) + own // 2]

    l_csrc.wait()
    l_nsrc.wait()
    l_coup.wait()

    @pl.when(has_prev)
    def _():
        for copy in ups:
            copy.wait_recv()

    @pl.when(out_prev)
    def _():
        for copy in downs:
            copy.start()

    @pl.when(has_next)
    def _():
        for copy in downs:
            copy.wait_recv()

    anchor = me * leaves - REACH
    last = leaves + 2 * REACH

    def spot(source):
        return jnp.where(source >= 0, jnp.clip(source - anchor, 0, last - 1), last)

    sums = []
    for t in range(leaves):
        picked = [wide_c[spot(csrc_s[t, a])] for a in range(slots_adm)]
        picked = [jnp.where(low, picked[a], picked[a + 1]) for a in range(0, slots_adm, 2)]
        field = mm(
            jnp.concatenate(picked, 1), coup_v[t].reshape(slots_adm * rank, rank)
        ).astype(BF16)
        inputs = [wide_x[spot(nsrc_s[t, n])] for n in range(1, slots_near)]
        sums.append(
            mm(jnp.concatenate(inputs, 1), near_v[t, 1:].reshape(-1, leaf))
            + first_v[:, t * leaf:(t + 1) * leaf]
            + mm(field, basis_v[t])
        )

    landed(part_in, lines - 1, r_recv.at[mine])
    for _, ok, here, _ in across:
        when(ok, functools.partial(landed, part_in, lines, r_recv.at[here]))
    total = jnp.zeros((rows, 2 * rank), F32)
    for j in range(part_in.shape[0]):
        term = part_in[j].astype(F32)
        if groups != 2 and j // lines != 1:
            term = jnp.where(group > 0 if j < lines else group < groups - 1, term, 0.0)
        total += term
    total = jnp.where(low == (own % 2 == 0), total, 0.0)
    far = mm(total.astype(BF16), spread_v[...])
    for t in range(leaves):
        out_ref[:, t * leaf:(t + 1) * leaf] = (
            sums[t] + far[:, t * leaf:(t + 1) * leaf]
        ).astype(BF16)

    for q in range(line):
        pl.when(q != rel)(lambda q=q: to_mate(q).wait_send())
    landed(part_in, lines - 1, r_send.at[0])
    for i, (_, ok, _, _) in enumerate(across):
        when(ok, functools.partial(landed, part_in, lines, r_send.at[i + 1]))

    @pl.when(has_next)
    def _():
        for copy in ups:
            copy.wait_send()

    @pl.when(has_prev)
    def _():
        for copy in downs:
            copy.wait_send()


def solution(mesh):
    shape = tuple(mesh.shape[a] for a in AXES)
    count = shape[0] * shape[1] * shape[2]

    def local(rhs, basis, trans, coup, csrc, near, nsrc, top, cc):
        leaves, rank, leaf = basis.shape
        rows = rhs.shape[0]
        gsize = 2 ** top.shape[0]
        lines = (2 if count == 2 * gsize else 3) * gsize // 2**LOW
        args = (rhs, basis, trans, coup, csrc, near, nsrc, top, cc)

        def room(x):
            kind = pltpu.SMEM if x.dtype == jnp.int32 else pltpu.VMEM
            return kind(x.shape, x.dtype)

        dma = pltpu.SemaphoreType.DMA
        return pl.pallas_call(
            functools.partial(kernel, shape),
            out_shape=pltpu.VMEM(rhs.shape, BF16),
            in_specs=[pl.BlockSpec(memory_space=pl.ANY)] * len(args),
            out_specs=pl.BlockSpec(memory_space=pltpu.VMEM),
            scratch_shapes=[room(x) for x in args] + [
                pltpu.VMEM((leaves + 2 * REACH + 1, rows, leaf), BF16),
                pltpu.VMEM((leaves + 2 * REACH + 1, rows, 2 * rank), BF16),
                pltpu.VMEM((2**LOW, rows, 2 * rank), BF16),
                pltpu.VMEM((lines // 2, rows, 2 * rank), BF16),
                pltpu.VMEM((lines, rows, 2 * rank), BF16),
                pltpu.VMEM((2**LOW * rank, lines * rank), BF16),
                pltpu.VMEM((2 * rank, leaves * leaf), BF16),
                pltpu.VMEM((rows, leaves * leaf), F32),
                dma((len(args),)), dma((4,)), dma((4,)), dma((2**LOW,)), dma((2**LOW,)),
                dma((3,)), dma((3,)),
            ],
            compiler_params=pltpu.CompilerParams(collective_id=0, has_side_effects=True),
        )(*(pltpu.with_memory_space_constraint(x, pltpu.HBM) for x in args))

    placed = (
        P(None, AXES),
        P(AXES, None, None),
        P(AXES, None, None),
        P(AXES, None, None, None),
        P(AXES, None),
        P(AXES, None, None, None),
        P(AXES, None),
        P(),
        P(),
    )
    return jax.shard_map(
        local, mesh=mesh, in_specs=placed, out_specs=P(None, AXES), check_vma=False
    )
```

```python
import functools

import jax
import jax.numpy as jnp
from jax import lax
from jax.experimental import pallas as pl
from jax.experimental.pallas import tpu as pltpu
from jax.sharding import PartitionSpec as P

AXES = ("gx", "gy", "gz")
REACH = 2
LOW = 2
MESH = pl.DeviceIdType.MESH
BF16 = jnp.bfloat16
F32 = jnp.float32


def mm(a, b):
    return jnp.dot(a, b, preferred_element_type=F32)


def mm_nt(a, b):
    return lax.dot_general(a, b, (((1,), (1,)), ((), ())), preferred_element_type=F32)


def mm_tn(a, b):
    return lax.dot_general(a, b, (((0,), (0,)), ((), ())), preferred_element_type=F32)


def kernel(
    shape,
    rhs_h, basis_h, trans_h, coup_h, csrc_h, near_h, nsrc_h, top_h, cc_h,
    out_ref,
    rhs_v, basis_v, trans_v, coup_v, csrc_s, near_v, nsrc_s, top_v, cc_v,
    wide_x, wide_c, slots, part, part_in, gather_v, spread_v, first_v,
    local_sem, halo_send, halo_recv, p_send, p_recv, r_send, r_recv,
):
    nx, ny, nz = shape
    count = nx * ny * nz
    leaves, rank, leaf = basis_v.shape
    rows = rhs_v.shape[0]
    slots_near = near_v.shape[1]
    slots_adm = coup_v.shape[1]
    topl = top_v.shape[0]
    gsize = 2**topl
    groups = count // gsize
    line = 2**LOW
    lines = gsize // line
    width = part.shape[0] * 2 * rank

    me = (lax.axis_index("gx") * ny + lax.axis_index("gy")) * nz + lax.axis_index("gz")
    group = me // gsize
    mine_line = me // line
    rel = me % line
    own = mine_line % lines

    def place(e):
        return (e // (ny * nz), (e // nz) % ny, e % nz)

    loads = []
    for i, (src, dst) in enumerate(
        (
            (rhs_h, rhs_v), (basis_h, basis_v), (trans_h, trans_v), (top_h, top_v),
            (cc_h, cc_v), (csrc_h, csrc_s), (nsrc_h, nsrc_s), (coup_h, coup_v),
            (near_h, near_v),
        )
    ):
        load = pltpu.make_async_copy(src, dst, local_sem.at[i])
        if i < 3:
            load.start()
        loads.append(load)
    (l_rhs, l_basis, l_trans, l_top, l_cc, l_csrc, l_nsrc, l_coup, l_near) = loads

    if groups == 2:
        mine = group
        across = ((1 - group, None, 1 - group, group),)
    else:
        mine = 1
        across = ((group - 1, group > 0, 0, 2), (group + 1, group < groups - 1, 2, 0))
    has_prev, has_next = me > 0, me < count - 1

    def when(cond, fn):
        if cond is None:
            fn()
        else:
            pl.when(cond)(fn)

    mates = [mine_line * line + (rel ^ r) for r in range(line - 1, 0, -1)]

    def each_line(fn):
        for i, (g, ok, here, there) in enumerate(across):
            def outer(i=i, g=g, here=here, there=there):
                for k in range(lines):
                    l = own ^ k
                    fn(g * gsize + l * line + rel, here, l, there, i + 1)
            when(ok, outer)
        for k in range(lines - 1, 0, -1):
            l = own ^ k
            fn(group * gsize + l * line + rel, mine, l, mine, 0)

    barrier = pltpu.get_barrier_semaphore()

    def greet(e, *_):
        pl.semaphore_signal(barrier, inc=1, device_id=place(e), device_id_type=MESH)

    for e in mates:
        greet(e)
    out_prev = has_prev & (rel == 0)
    out_next = has_next & (rel == line - 1)
    when(out_prev, functools.partial(greet, me - 1))
    when(out_next, functools.partial(greet, me + 1))
    each_line(greet)
    expected = jnp.int32(line - 1 + lines - 1)
    expected += out_prev.astype(jnp.int32) + out_next.astype(jnp.int32)
    for _, ok, _, _ in across:
        expected += lines if ok is None else lines * ok.astype(jnp.int32)

    wide_x[leaves + 2 * REACH] = jnp.zeros((rows, leaf), BF16)
    wide_c[leaves + 2 * REACH] = jnp.zeros((rows, 2 * rank), BF16)
    low = lax.broadcasted_iota(jnp.int32, (rows, 2 * rank), 1) < rank

    l_rhs.wait()
    l_basis.wait()
    coeffs = []
    for t in range(leaves):
        block = rhs_v[:, t * leaf:(t + 1) * leaf]
        wide_x[REACH + t] = block
        basis = basis_v[t]
        both = mm_nt(block, jnp.concatenate([basis, basis], 0)).astype(BF16)
        wide_c[REACH + t] = both
        coeffs.append(both)
    pairs = [jnp.where(low, coeffs[t], coeffs[t + 1]) for t in range(0, leaves, 2)]
    l_trans.wait()
    root = mm(jnp.concatenate(pairs, 1), trans_v[...].reshape(leaves * rank, rank)).astype(BF16)
    slots[rel] = jnp.concatenate([root, root], 1)

    def halo(buf, i, up):
        first, land = (leaves, 0) if up else (REACH, leaves + REACH)
        return pltpu.make_async_remote_copy(
            src_ref=buf.at[pl.ds(first, REACH)], dst_ref=buf.at[pl.ds(land, REACH)],
            send_sem=halo_send.at[i], recv_sem=halo_recv.at[i],
            device_id=place(me + 1 if up else me - 1), device_id_type=MESH,
        )

    ups = (halo(wide_c, 0, True), halo(wide_x, 1, True))
    downs = (halo(wide_c, 2, False), halo(wide_x, 3, False))

    def send():
        pl.semaphore_wait(barrier, expected)

        for e in mates:
            pltpu.make_async_remote_copy(
                src_ref=slots.at[rel], dst_ref=slots.at[rel],
                send_sem=p_send.at[0], recv_sem=p_recv.at[0],
                device_id=place(e), device_id_type=MESH,
            ).start()
        @pl.when(has_next)
        def _():
            for copy in ups:
                copy.start()

        @pl.when(has_prev)
        def _():
            for copy in downs:
                copy.start()

    def prepare():
        for load in loads[3:]:
            load.start()
        l_top.wait()
        l_cc.wait()
        lane_block = lax.broadcasted_iota(jnp.int32, (1, width), 1) // rank
        lane_group = lane_block // lines
        if groups != 2:
            lane_group = lane_group + (group - 1)
        dest = lane_group * gsize + (lane_block % lines) * line + rel
        row = lax.broadcasted_iota(jnp.int32, (rank, rank), 0)
        col = lax.broadcasted_iota(jnp.int32, (rank, rank), 1)
        down = jnp.where(row == col, 1.0, 0.0).astype(BF16)
        reach_mats = []
        for h in range(topl + 1):
            if h == 1:
                down = top_v[0, rel % 2]
            elif 1 < h <= LOW:
                down = mm(down, top_v[h - 1, (rel // 2 ** (h - 1)) % 2]).astype(BF16)
            elif h > LOW:
                down = jnp.concatenate([mm(down, top_v[h - 1, p]) for p in range(2)], 0).astype(BF16)
            stack = down if h > LOW else jnp.concatenate([down, down], 0)
            mat = mm_nt(cc_v[h].reshape(2 * rank, rank), stack)
            reach_mats.append(jnp.concatenate([mat] * (width // mat.shape[1]), 1))

        def coupled(h, cluster):
            home = dest >> h
            return jnp.where(cluster == home - 1, reach_mats[h][:rank], 0.0) + jnp.where(
                cluster == home + 1, reach_mats[h][rank:], 0.0
            )

        level = [coupled(topl, group)]
        for h in range(topl - 1, -1, -1):
            wide = jnp.concatenate([m.astype(BF16) for m in level], 1)
            if h >= LOW:
                level = [mm(top_v[h, (me >> h) % 2], wide) + coupled(h, me >> h)]
                continue
            grown = mm(top_v[h].reshape(2 * rank, rank), wide)
            level = [
                grown[(c % 2) * rank:(c % 2 + 1) * rank, (c // 2) * width:(c // 2 + 1) * width]
                + coupled(h, mine_line * 2 ** (LOW - h) + c)
                for c in range(2 ** (LOW - h))
            ]
        for c, m in enumerate(level):
            gather_v[c * rank:(c + 1) * rank] = m.astype(BF16)

        for t in range(leaves):
            mat = mm_tn(trans_v[t], basis_v[t]).astype(BF16)
            spread_v[:rank, t * leaf:(t + 1) * leaf] = mat
            spread_v[rank:, t * leaf:(t + 1) * leaf] = mat
        l_near.wait()
        for t in range(leaves):
            first_v[:, t * leaf:(t + 1) * leaf] = mm(wide_x[REACH + t], near_v[t, 0])

    turn = jnp.where(rel < line // 2, 0, 1)

    def step(i, carry):
        pl.when(i == turn)(prepare)
        pl.when(i != turn)(send)
        return carry

    lax.fori_loop(0, 2, step, 0)

    def landed(buf, number, sem):
        some = buf.at[pl.ds(0, number)]
        pltpu.make_async_copy(some, some, sem).wait()

    landed(slots, line - 1, p_recv.at[0])
    held = [jnp.where(low, slots[c], slots[c + 1]) for c in range(0, line, 2)]
    parts = mm(jnp.concatenate(held, 1), gather_v[...])
    for i in range(part.shape[0]):
        part[i] = parts[:, i * 2 * rank:(i + 1) * 2 * rank].astype(BF16)
    each_line(
        lambda e, here, l, there, i: pltpu.make_async_remote_copy(
            src_ref=part.at[here * (lines // 2) + l // 2], dst_ref=part_in.at[there * lines + own],
            send_sem=r_send.at[i], recv_sem=r_recv.at[there],
            device_id=place(e), device_id_type=MESH,
        ).start()
    )
    part_in[mine * lines + own] = part[mine * (lines // 2) + own // 2]

    l_csrc.wait()
    l_nsrc.wait()
    l_coup.wait()

    @pl.when(has_prev)
    def _():
        for copy in ups:
            copy.wait_recv()

    @pl.when(has_next)
    def _():
        for copy in downs:
            copy.wait_recv()

    anchor = me * leaves - REACH
    last = leaves + 2 * REACH

    def spot(source):
        return jnp.where(source >= 0, jnp.clip(source - anchor, 0, last - 1), last)

    sums = []
    for t in range(leaves):
        picked = [wide_c[spot(csrc_s[t, a])] for a in range(slots_adm)]
        picked = [jnp.where(low, picked[a], picked[a + 1]) for a in range(0, slots_adm, 2)]
        field = mm(
            jnp.concatenate(picked, 1), coup_v[t].reshape(slots_adm * rank, rank)
        ).astype(BF16)
        inputs = [wide_x[spot(nsrc_s[t, n])] for n in range(1, slots_near)]
        sums.append(
            mm(jnp.concatenate(inputs, 1), near_v[t, 1:].reshape(-1, leaf))
            + first_v[:, t * leaf:(t + 1) * leaf]
            + mm(field, basis_v[t])
        )

    landed(part_in, lines - 1, r_recv.at[mine])
    for _, ok, here, _ in across:
        when(ok, functools.partial(landed, part_in, lines, r_recv.at[here]))
    total = jnp.zeros((rows, 2 * rank), F32)
    for j in range(part_in.shape[0]):
        term = part_in[j].astype(F32)
        if groups != 2 and j // lines != 1:
            term = jnp.where(group > 0 if j < lines else group < groups - 1, term, 0.0)
        total += term
    total = jnp.where(low == (own % 2 == 0), total, 0.0)
    far = mm(total.astype(BF16), spread_v[...])
    for t in range(leaves):
        out_ref[:, t * leaf:(t + 1) * leaf] = (
            sums[t] + far[:, t * leaf:(t + 1) * leaf]
        ).astype(BF16)

    landed(slots, line - 1, p_send.at[0])
    landed(part_in, lines - 1, r_send.at[0])
    for i, (_, ok, _, _) in enumerate(across):
        when(ok, functools.partial(landed, part_in, lines, r_send.at[i + 1]))

    @pl.when(has_next)
    def _():
        for copy in ups:
            copy.wait_send()

    @pl.when(has_prev)
    def _():
        for copy in downs:
            copy.wait_send()


def solution(mesh):
    shape = tuple(mesh.shape[a] for a in AXES)
    count = shape[0] * shape[1] * shape[2]

    def local(rhs, basis, trans, coup, csrc, near, nsrc, top, cc):
        leaves, rank, leaf = basis.shape
        rows = rhs.shape[0]
        gsize = 2 ** top.shape[0]
        lines = (2 if count == 2 * gsize else 3) * gsize // 2**LOW
        args = (rhs, basis, trans, coup, csrc, near, nsrc, top, cc)

        def room(x):
            kind = pltpu.SMEM if x.dtype == jnp.int32 else pltpu.VMEM
            return kind(x.shape, x.dtype)

        dma = pltpu.SemaphoreType.DMA
        return pl.pallas_call(
            functools.partial(kernel, shape),
            out_shape=pltpu.VMEM(rhs.shape, BF16),
            in_specs=[pl.BlockSpec(memory_space=pl.ANY)] * len(args),
            out_specs=pl.BlockSpec(memory_space=pltpu.VMEM),
            scratch_shapes=[room(x) for x in args] + [
                pltpu.VMEM((leaves + 2 * REACH + 1, rows, leaf), BF16),
                pltpu.VMEM((leaves + 2 * REACH + 1, rows, 2 * rank), BF16),
                pltpu.VMEM((2**LOW, rows, 2 * rank), BF16),
                pltpu.VMEM((lines // 2, rows, 2 * rank), BF16),
                pltpu.VMEM((lines, rows, 2 * rank), BF16),
                pltpu.VMEM((2**LOW * rank, lines * rank), BF16),
                pltpu.VMEM((2 * rank, leaves * leaf), BF16),
                pltpu.VMEM((rows, leaves * leaf), F32),
                dma((len(args),)), dma((4,)), dma((4,)), dma((1,)), dma((1,)),
                dma((3,)), dma((3,)),
            ],
            compiler_params=pltpu.CompilerParams(collective_id=0, has_side_effects=True),
        )(*(pltpu.with_memory_space_constraint(x, pltpu.HBM) for x in args))

    placed = (
        P(None, AXES),
        P(AXES, None, None),
        P(AXES, None, None),
        P(AXES, None, None, None),
        P(AXES, None),
        P(AXES, None, None, None),
        P(AXES, None),
        P(),
        P(),
    )
    return jax.shard_map(
        local, mesh=mesh, in_specs=placed, out_specs=P(None, AXES), check_vma=False
    )
```
